512 devices in a mesh: rep: 16 (over z, core), seq: 32 (over x, y).
Axes of the slice: x: 4, y: 8, z: 8, core: 2. Of those that a mesh axis runs over, the one named last changes fastest.
Arguments:
- normed_input: bfloat16 [16, 4096, 4096], P('rep', 'seq'), may hold values from -6 to 6
- document_index: int32 [16, 4096], P('rep', 'seq'), may hold values from 0 to 63, never falling along the last dimension, each value on 1 to 897 neighbouring positions
- frozen_query_state: bfloat16 [16, 4096, 2048], P('rep', 'seq'), may hold values from -5 to 5
- frozen_keyvalue_weight: bfloat16 [16, 4096, 1024], P('rep', 'seq'), may hold values from -5 to 5
- layer_output_gradient: bfloat16 [16, 4096, 4096], P('rep', 'seq'), may hold values from -0.75 to 0.75
- frozen_output_gradient: bfloat16 [16, 4096, 2048], P('rep', 'seq'), may hold values from -0.75 to 0.75
- adapter_down_weight: bfloat16 [3, 4096, 16], replicated, may hold values from -0.09375 to 0.09375
- query_up_weight: bfloat16 [16, 2048], replicated, may hold values from -1.5 to 1.5
- keyvalue_up_weight: bfloat16 [2, 16, 512], replicated, may hold values from -1.5 to 1.5
- output_down_weight: bfloat16 [2048, 16], replicated, may hold values from -0.125 to 0.125
- output_up_weight: bfloat16 [16, 4096], replicated, may hold values from -1.5 to 1.5
Outputs:
- grad_lora_down: bfloat16 [3, 4096, 16], replicated
- grad_query_up: bfloat16 [16, 2048], replicated
- grad_keyval_up: bfloat16 [2, 16, 512], replicated
- grad_output_down: bfloat16 [2048, 16], replicated
- grad_output_up: bfloat16 [16, 4096], replicated
The draws below stay inside these ranges and needn't reach their ends.
Inputs may be any that keep to these rules, and one draw needn't show every extreme that they name: document_index never fall along a sequence; each document holds 1 to 897 consecutive positions, and one holds exactly 897.
All inputs are finite; a program needn't handle non-finite values.
Results may differ from the reference program's by a relative error of at most 0.03.
Values may be sent and summed in bfloat16 or wider, within the bound.
No kernel may reach another device: no remote copies, remote signals or barrier semaphores. Data moves between devices by JAX's collectives and lax.ppermute only.
A program may use at most 128 MiB of HBM per device.

```python
import math
import jax
import jax.numpy as jnp
import numpy as np
from jax import lax

MODEL_WIDTH = 4096
QUERY_HEADS = 16
KEY_HEADS = 4
HEAD_SIZE = 128
ADAPTER_RANK = 16
TOK_DEV = 128
QW = 2048
KEY_COLUMNS = 512
SEQS = 16
LEN = 4096
SPAN = 8
MOST = 897
DOCS = 64


def draw_frozen_query_state(key, part):
    key = jax.random.fold_in(key, 11)
    result = jax.random.truncated_normal(key, -5.0, 5.0, (SEQS, LEN, QW), jnp.float32)
    return result.astype(jnp.bfloat16)


def draw_frozen_keyvalue_weight(key, part):
    key = jax.random.fold_in(key, 13)
    result = jax.random.truncated_normal(key, -5.0, 5.0, (SEQS, LEN, 2 * KEY_COLUMNS), jnp.float32)
    return result.astype(jnp.bfloat16)


def block_scale(own_key, dims, cuts, least, largest):
    def one(dim, shards_of):
        heights = jax.random.uniform(jax.random.fold_in(jax.random.fold_in(own_key, 6), dim), (shards_of,), jnp.float32, least / len(cuts), largest / len(cuts))
        return jnp.repeat(jnp.exp(heights), dims[dim] // shards_of).reshape((-1,) + (1,) * (len(dims) - dim - 1))

    loudness = one(*cuts[0])
    for cut in cuts[1:]:
        loudness = loudness * one(*cut)
    return loudness


def length_profile(count, total, most, lean):
    loads = [(1 << 20) // math.isqrt(standing ** lean) + 1 for standing in range(2, count + 1)]
    spare, given = total - most - (count - 1), [1] * (count - 1)
    while spare > 0:
        free = [i for i in range(count - 1) if given[i] < most]
        pool, budget = sum([loads[i] for i in free]), spare
        for i in free:
            addition = min(most - given[i], max(1, budget * loads[i] // pool), spare)
            given[i] = given[i] + addition
            spare = spare - addition
    return np.array([most] + given)


def uneven_parts(stream_key, count, total, bound, slope):
    if count == 2:
        one = jax.random.randint(stream_key, (), max(1, total - bound), min(bound, total - 1) + 1)
        return jnp.stack([one, total - one])
    lengths = jnp.asarray(length_profile(count, total, bound, slope), jnp.int32)
    couples = (count - 1) // 2
    source_of, sink = lengths[1:1 + 2 * couples:2], lengths[2:2 + 2 * couples:2]
    margin = jnp.minimum(source_of - 1, bound - sink)
    passed = jax.random.randint(jax.random.fold_in(stream_key, 1), (couples,), 0, 1 << 20) % (margin + 1)
    lengths = lengths.at[1:1 + 2 * couples:2].set(source_of - passed).at[2:2 + 2 * couples:2].set(sink + passed)
    return lengths[jax.random.permutation(jax.random.fold_in(stream_key, 2), count)]


def noise(key, extent, deviation, reach, split=(), held_as=jnp.bfloat16):
    loudness = block_scale(key, extent, split, -0.22, 0.18) if split else 1.0
    entries = jax.random.normal(key, extent, jnp.float32) * deviation * loudness
    return jnp.minimum(jnp.maximum(entries, -reach), reach).astype(held_as)


def setup_inputs(seed: int = 0) -> dict:
    seeds = jax.random.split(jax.random.key(seed), 12)
    normed_input = noise(seeds[0], (SEQS, LEN, MODEL_WIDTH), 1.0, 6.0, ((0, 16), (1, 32)))
    document_index = jax.vmap(lambda own: jnp.searchsorted(jnp.cumsum(uneven_parts(own, DOCS, LEN, MOST, 2)), jnp.arange(LEN), side="right"))(jax.random.split(seeds[1], SEQS)).reshape((SEQS, LEN)).astype(jnp.int32)
    frozen_query_state = draw_frozen_query_state(jax.random.fold_in(seeds[11], 71), 0)
    frozen_keyvalue_weight = draw_frozen_keyvalue_weight(jax.random.fold_in(seeds[11], 71), 0)
    layer_output_gradient = noise(seeds[4], (SEQS, LEN, MODEL_WIDTH), 0.05, 0.75, ((0, 16), (1, 32)))
    frozen_output_gradient = noise(seeds[5], (SEQS, LEN, QW), 0.05, 0.75, ((0, 16), (1, 32)))
    adapter_down_weight = noise(seeds[6], (3, MODEL_WIDTH, ADAPTER_RANK), MODEL_WIDTH ** -0.5, 0.09375)
    query_up_weight = noise(seeds[7], (ADAPTER_RANK, QW), ADAPTER_RANK ** -0.5, 1.5)
    keyvalue_up_weight = noise(seeds[8], (2, ADAPTER_RANK, KEY_COLUMNS), ADAPTER_RANK ** -0.5, 1.5)
    output_down_weight = noise(seeds[9], (QW, ADAPTER_RANK), QW ** -0.5, 0.125)
    output_up_weight = noise(seeds[10], (ADAPTER_RANK, MODEL_WIDTH), ADAPTER_RANK ** -0.5, 1.5)
    return dict(normed_input=normed_input, document_index=document_index, frozen_query_state=frozen_query_state, frozen_keyvalue_weight=frozen_keyvalue_weight, layer_output_gradient=layer_output_gradient, frozen_output_gradient=frozen_output_gradient, adapter_down_weight=adapter_down_weight, query_up_weight=query_up_weight, keyvalue_up_weight=keyvalue_up_weight, output_down_weight=output_down_weight, output_up_weight=output_up_weight)


def cast_to_bfloat16(values):
    return lax.optimization_barrier(values.astype(jnp.bfloat16))


def reference(normed_input, document_index, frozen_query_state, frozen_keyvalue_weight, layer_output_gradient, frozen_output_gradient, adapter_down_weight, query_up_weight, keyvalue_up_weight, output_down_weight, output_up_weight):
    group_factor = QUERY_HEADS // KEY_HEADS
    inverse = 1.0 / (HEAD_SIZE ** 0.5)
    query_block_size = 4 * TOK_DEV
    key_width = min(LEN, query_block_size + SPAN * TOK_DEV)
    nblocks = LEN // query_block_size

    def one_sequence(totals, inputs):
        hidden_state, documents, query_rows, keyval_rows, outgrad, frozen_rows = inputs
        low_rank_state = cast_to_bfloat16(jnp.einsum('hy,wym->whm', hidden_state.astype(jnp.float32), adapter_down_weight.astype(jnp.float32)))
        query_matrix = cast_to_bfloat16(query_rows.astype(jnp.float32) + 0.5 * jnp.dot(low_rank_state[0], query_up_weight, preferred_element_type=jnp.float32))
        key_delta = jnp.dot(low_rank_state[1], keyvalue_up_weight[0], preferred_element_type=jnp.float32)
        value_delta = jnp.dot(low_rank_state[2], keyvalue_up_weight[1], preferred_element_type=jnp.float32)
        keyvals = cast_to_bfloat16(keyval_rows.astype(jnp.float32) + 0.5 * jnp.concatenate([key_delta, value_delta], axis=1))
        back_out = cast_to_bfloat16(jnp.dot(outgrad, output_up_weight.T, preferred_element_type=jnp.float32))
        attention_gradient = cast_to_bfloat16(frozen_rows.astype(jnp.float32) + 0.5 * jnp.dot(back_out, output_down_weight.T, preferred_element_type=jnp.float32))

        def one_block(dkv_total, block):
            query_start_index = (block * query_block_size).astype(jnp.int32)
            kstart = jnp.maximum(query_start_index + query_block_size - key_width, 0).astype(jnp.int32)
            query_head_rows = lax.dynamic_slice_in_dim(query_matrix, query_start_index, query_block_size, 0).astype(jnp.float32).reshape(query_block_size, KEY_HEADS, group_factor, HEAD_SIZE)
            keyvalue_row_block = lax.dynamic_slice_in_dim(keyvals, kstart, key_width, 0).astype(jnp.float32)
            key_head_rows = keyvalue_row_block[:, :KEY_COLUMNS].reshape(key_width, KEY_HEADS, HEAD_SIZE)
            value_head_rows = keyvalue_row_block[:, KEY_COLUMNS:].reshape(key_width, KEY_HEADS, HEAD_SIZE)
            query_docs = lax.dynamic_slice_in_dim(documents, query_start_index, query_block_size, 0)
            key_docs = lax.dynamic_slice_in_dim(documents, kstart, key_width, 0)
            query_pos = query_start_index + jnp.arange(query_block_size, dtype=jnp.int32)
            key_pos = kstart + jnp.arange(key_width, dtype=jnp.int32)
            visible = (query_docs[:, None] == key_docs[None, :]) & (key_pos[None, :] <= query_pos[:, None])
            scores = jnp.einsum('pagd,kad->agpk', query_head_rows, key_head_rows) * inverse
            scores = jnp.where(visible[None, None], scores, -1e30)
            maxima = jnp.max(scores, axis=-1, keepdims=True)
            exponentials = jnp.exp(scores - maxima)
            softmax_probs = cast_to_bfloat16(exponentials / jnp.sum(exponentials, axis=-1, keepdims=True)).astype(jnp.float32)
            attn_rows = cast_to_bfloat16(jnp.einsum('agpk,kad->pagd', softmax_probs, value_head_rows))
            gradient_heads = lax.dynamic_slice_in_dim(attention_gradient, query_start_index, query_block_size, 0).astype(jnp.float32).reshape(query_block_size, KEY_HEADS, group_factor, HEAD_SIZE)
            deltas = jnp.einsum('pagd,pagd->agp', gradient_heads, attn_rows.astype(jnp.float32))
            dprobs = jnp.einsum('pagd,kad->agpk', gradient_heads, value_head_rows)
            dscores = cast_to_bfloat16(softmax_probs * (dprobs - deltas[..., None]) * inverse).astype(jnp.float32)
            dquery_rows = cast_to_bfloat16(jnp.einsum('agpk,kad->pagd', dscores, key_head_rows)).reshape(query_block_size, QW)
            dkey_rows = jnp.einsum('agpk,pagd->kad', dscores, query_head_rows).reshape(key_width, KEY_COLUMNS)
            dvalue_rows = jnp.einsum('agpk,pagd->kad', softmax_probs, gradient_heads).reshape(key_width, KEY_COLUMNS)
            current = lax.dynamic_slice(dkv_total, (kstart, jnp.int32(0)), (key_width, 2 * KEY_COLUMNS))
            dkv_total = lax.dynamic_update_slice(dkv_total, current + jnp.concatenate([dkey_rows, dvalue_rows], axis=1), (kstart, jnp.int32(0)))
            return dkv_total, (attn_rows.reshape(query_block_size, QW), dquery_rows)

        dkv_total, (attn_blocks, dquery_blocks) = lax.scan(one_block, jnp.zeros((LEN, 2 * KEY_COLUMNS), jnp.float32), jnp.arange(nblocks, dtype=jnp.int32))
        attended = attn_blocks.reshape(LEN, QW)
        dqueries = dquery_blocks.reshape(LEN, QW)
        dkeyvals = cast_to_bfloat16(dkv_total)
        back_query = cast_to_bfloat16(jnp.dot(dqueries, query_up_weight.T, preferred_element_type=jnp.float32))
        back_key = cast_to_bfloat16(jnp.dot(dkeyvals[:, :KEY_COLUMNS], keyvalue_up_weight[0].T, preferred_element_type=jnp.float32))
        back_value = cast_to_bfloat16(jnp.dot(dkeyvals[:, KEY_COLUMNS:], keyvalue_up_weight[1].T, preferred_element_type=jnp.float32))
        hidden_f = hidden_state.astype(jnp.float32)
        term_down = jnp.stack([jnp.einsum('td,tr->dr', hidden_f, piece.astype(jnp.float32)) for piece in (back_query, back_key, back_value)])
        term_query_up = jnp.einsum('tr,tc->rc', low_rank_state[0].astype(jnp.float32), dqueries.astype(jnp.float32))
        term_keyval_up = jnp.stack([
            jnp.einsum('tr,tc->rc', low_rank_state[1].astype(jnp.float32), dkeyvals[:, :KEY_COLUMNS].astype(jnp.float32)),
            jnp.einsum('tr,tc->rc', low_rank_state[2].astype(jnp.float32), dkeyvals[:, KEY_COLUMNS:].astype(jnp.float32))])
        low_out = cast_to_bfloat16(jnp.dot(attended, output_down_weight, preferred_element_type=jnp.float32))
        term_output_down = jnp.einsum('tc,tr->cr', attended.astype(jnp.float32), back_out.astype(jnp.float32))
        term_output_up = jnp.einsum('tr,td->rd', low_out.astype(jnp.float32), outgrad.astype(jnp.float32))
        terms = (term_down, term_query_up, term_keyval_up, term_output_down, term_output_up)
        return tuple(total + term for total, term in zip(totals, terms)), None

    zeros = (jnp.zeros((3, MODEL_WIDTH, ADAPTER_RANK), jnp.float32), jnp.zeros((ADAPTER_RANK, QW), jnp.float32), jnp.zeros((2, ADAPTER_RANK, KEY_COLUMNS), jnp.float32),
             jnp.zeros((QW, ADAPTER_RANK), jnp.float32), jnp.zeros((ADAPTER_RANK, MODEL_WIDTH), jnp.float32))
    totals, _ = lax.scan(one_sequence, zeros, (normed_input, document_index, frozen_query_state, frozen_keyvalue_weight, layer_output_gradient, frozen_output_gradient))
    factor = 0.5 / SEQS
    return ((factor * totals[0]).astype(jnp.bfloat16), (factor * totals[1]).astype(jnp.bfloat16),
            (factor * totals[2]).astype(jnp.bfloat16), (factor * totals[3]).astype(jnp.bfloat16),
            (factor * totals[4]).astype(jnp.bfloat16))
```

```python
import jax
import jax.numpy as jnp
from jax import lax
from jax.experimental import pallas as pl
from jax.experimental.pallas import tpu as pltpu
from jax.sharding import Mesh, PartitionSpec as P

QUERY_HEADS = 16
KEY_HEADS = 4
HEAD_SIZE = 128
KEY_COLUMNS = 512
ROWS = 128
RANK = 16
SPAN = 8
GROUP = QUERY_HEADS // KEY_HEADS
WIDTH = 4096
QUERY_COLUMNS = QUERY_HEADS * HEAD_SIZE
PACK_ROWS = ROWS + 16
BF = jnp.bfloat16
F32 = jnp.float32
INVERSE = 1.0 / HEAD_SIZE**0.5

NT = (((1,), (1,)), ((), ()))
TN = (((0,), (0,)), ((), ()))
NN = (((1,), (0,)), ((), ()))


def dot(a, b, dims=NN):
    return lax.dot_general(a, b, dims, preferred_element_type=F32)


def keyval_kernel(x_ref, down_ref, keyval_ref, up_ref, doc_ref, low_ref, pack_ref):
    low = dot(down_ref[...], x_ref[...], NT).astype(BF)
    low_ref[...] = low
    for c in range(2):
        part = pl.ds(c * KEY_COLUMNS, KEY_COLUMNS)
        delta = dot(low[(c + 1) * RANK : (c + 2) * RANK], up_ref[c], TN)
        pack_ref[pl.ds(0, ROWS), part] = (
            keyval_ref[:, part].astype(F32) + 0.5 * delta
        ).astype(BF)
    documents = jnp.broadcast_to(doc_ref[...].astype(F32), (RANK, ROWS)).astype(BF)
    pack_ref[pl.ds(ROWS, RANK), :] = jnp.concatenate(
        [low[RANK : 2 * RANK], low[2 * RANK :], documents, jnp.zeros((RANK, 5 * ROWS), BF)], axis=1
    )


def query_kernel(low_ref, query_ref, query_up_ref, outgrad_ref, out_up_ref, frozen_ref, out_down_ref,
                 q_ref, grad_ref, back_out_ref):
    q_ref[...] = (
        query_ref[...].astype(F32) + 0.5 * dot(low_ref[pl.ds(0, RANK), :], query_up_ref[...], TN)
    ).astype(BF)
    back_out = dot(out_up_ref[...], outgrad_ref[...], NT).astype(BF)
    back_out_ref[...] = back_out
    grad_ref[...] = (
        frozen_ref[...].astype(F32) + 0.5 * dot(back_out, out_down_ref[...], TN)
    ).astype(BF)


def attention_kernel(place_ref, doc_ref, low_ref, q_ref, grad_ref, back_out_ref, query_up_ref, up_ref,
                     out_down_ref, *rest):
    blocks = rest[:SPAN]
    parts_ref, back_query_ref, low_out_ref, query_term_ref, keyval_term_ref, out_term_ref = rest[
        SPAN : SPAN + 6
    ]
    bias, keys, values, low_keys, low_values, back_parts = rest[SPAN + 6 :]
    position, column = place_ref[0], place_ref[1]
    own = jnp.transpose(jnp.broadcast_to(doc_ref[...].astype(F32), (ROWS, ROWS)))
    row = lax.broadcasted_iota(jnp.int32, (ROWS, ROWS), 0)
    col = lax.broadcasted_iota(jnp.int32, (ROWS, ROWS), 1)
    for o in range(SPAN):
        span = pl.ds(o * ROWS, ROWS)
        extra = blocks[o][pl.ds(ROWS, RANK), :]
        low_keys[:, span] = extra[:, :ROWS]
        low_values[:, span] = extra[:, ROWS : 2 * ROWS]
        document = jnp.broadcast_to(extra[:1, 2 * ROWS : 3 * ROWS].astype(F32), (ROWS, ROWS))
        seen = own == document
        if o == 0:
            seen = seen & (col <= row)
        else:
            seen = seen & (jnp.broadcast_to(position, (ROWS, ROWS)) >= o)
        bias[:, span] = jnp.where(seen, 0.0, -1e30)
    back_parts[...] = jnp.zeros_like(back_parts)
    low_zero = low_ref[pl.ds(0, RANK), :]
    back_out = back_out_ref[...]

    def one_group(g, sums):
        back_query, low_out = sums
        at = pl.ds(pl.multiple_of(g * HEAD_SIZE, HEAD_SIZE), HEAD_SIZE)
        value_at = pl.ds(pl.multiple_of(KEY_COLUMNS + g * HEAD_SIZE, HEAD_SIZE), HEAD_SIZE)
        for o in range(SPAN):
            span = pl.ds(o * ROWS, ROWS)
            keys[span, :] = blocks[o][pl.ds(0, ROWS), at]
            values[span, :] = blocks[o][pl.ds(0, ROWS), value_at]
        heads = [
            pl.ds(pl.multiple_of((g * GROUP + i) * HEAD_SIZE, HEAD_SIZE), HEAD_SIZE)
            for i in range(GROUP)
        ]
        q = jnp.concatenate([q_ref[:, h] for h in heads], axis=0)
        grad = jnp.concatenate([grad_ref[:, h] for h in heads], axis=0)
        k, v = keys[...], values[...]
        scores = dot(q, k, NT).reshape(GROUP, ROWS, SPAN * ROWS) * INVERSE + bias[...][None]
        scores = scores.reshape(GROUP * ROWS, SPAN * ROWS)
        powers = jnp.exp(scores - jnp.max(scores, axis=-1, keepdims=True))
        probs = (powers * (1.0 / jnp.sum(powers, axis=-1, keepdims=True))).astype(BF)
        attn = dot(probs, v).astype(BF)
        delta = jnp.sum(grad.astype(F32) * attn.astype(F32), axis=-1, keepdims=True)
        dprobs = dot(grad, v, NT)
        dscores = (probs.astype(F32) * ((dprobs - delta) * INVERSE)).astype(BF)
        dq = dot(dscores, k).astype(BF)
        dkeys = dot(q, dscores, TN).astype(BF)
        dvalues = dot(grad, probs, TN).astype(BF)
        back_parts[pl.ds(0, RANK), :] += dot(up_ref[0, :, at], dkeys)
        back_parts[pl.ds(RANK, RANK), :] += dot(up_ref[1, :, at], dvalues)
        keyval_term_ref[pl.ds(0, RANK), at] = dot(low_keys[...], dkeys, NT)
        keyval_term_ref[pl.ds(RANK, RANK), at] = dot(low_values[...], dvalues, NT)
        for i, h in enumerate(heads):
            mine = slice(i * ROWS, (i + 1) * ROWS)
            query_term_ref[:, h] = dot(low_zero, dq[mine])
            out_term_ref[:, h] = dot(back_out, attn[mine])
            back_query = back_query + dot(query_up_ref[:, h], dq[mine], NT)
            low_out = low_out + dot(out_down_ref[:, h], attn[mine], NT)
        return back_query, low_out

    zero = jnp.zeros((RANK, ROWS), F32)
    back_query, low_out = lax.fori_loop(0, KEY_HEADS, one_group, (zero, zero))
    back_query_ref[...] = back_query.astype(BF)
    low_out_ref[...] = low_out.astype(BF)
    for o in range(SPAN):
        parts_ref[lax.rem(column + (SPAN - o), SPAN)] = back_parts[:, pl.ds(o * ROWS, ROWS)].astype(BF)


def term_kernel(place_ref, x_ref, outgrad_ref, back_query_ref, here_ref, there_ref, low_out_ref,
                query_term_ref, keyval_term_ref, out_term_ref, kept_ref, sent_ref, both):
    core = place_ref[2]
    back_keyval = (here_ref[...] + there_ref[...].astype(F32)).astype(BF)
    back = jnp.concatenate([back_query_ref[...], back_keyval], axis=0)
    down = dot(back, x_ref[...]).astype(BF)
    up = dot(low_out_ref[...], outgrad_ref[...]).astype(BF)
    query_term = query_term_ref[...].astype(BF)
    keyval_term = keyval_term_ref[...].astype(BF)
    out_term = out_term_ref[...].astype(BF)

    def put(half, tile, value):
        both[half, tile // 3, pl.ds(tile % 3 * RANK, RANK), :] = value

    def tiles(half, first, array):
        for t in range(array.shape[1] // ROWS):
            put(half, first + t, array[:, t * ROWS : (t + 1) * ROWS])
        return first + array.shape[1] // ROWS

    first = 0
    for c in range(3):
        first = tiles(0, first, down[c * RANK : (c + 1) * RANK])
    first = tiles(1, 0, query_term)
    first = tiles(1, first, keyval_term[:RANK])
    first = tiles(1, first, keyval_term[RANK:])
    first = tiles(1, first, out_term)
    first = tiles(1, first, up)
    for t in range(first, 96):
        put(1, t, jnp.zeros((RANK, ROWS), BF))
    kept_ref[...] = both[core]
    sent_ref[...] = both[1 - core]


def unpack_kernel(place_ref, kept_ref, sent_ref, down_ref, query_ref, keyval_ref, out_down_ref, out_up_ref, both):
    core = place_ref[2]
    both[core] = kept_ref[...]
    both[1 - core] = sent_ref[...]

    def get(half, tile):
        return both[half, tile // 3, pl.ds(tile % 3 * RANK, RANK), :]

    for c in range(3):
        for t in range(WIDTH // ROWS):
            down_ref[c, :, pl.ds(t * ROWS, ROWS)] = get(0, c * (WIDTH // ROWS) + t)
    first = 0
    for ref, lead in ((query_ref, None), (keyval_ref, 0), (keyval_ref, 1), (out_down_ref, None), (out_up_ref, None)):
        count = ref.shape[-1] // ROWS
        for t in range(count):
            if lead is None:
                ref[:, pl.ds(t * ROWS, ROWS)] = get(1, first + t)
            else:
                ref[lead, :, pl.ds(t * ROWS, ROWS)] = get(1, first + t)
        first += count


VMEM = pl.BlockSpec(memory_space=pltpu.VMEM)
SMEM = pl.BlockSpec(memory_space=pltpu.SMEM)


def call(kernel, name, outs, args, scratch=(), flops=0, size=0, smem_first=False, limit=32 << 20):
    specs = [SMEM if smem_first and i == 0 else VMEM for i in range(len(args))]
    return pl.pallas_call(
        kernel,
        name=name,
        out_shape=outs,
        in_specs=specs,
        out_specs=jax.tree.map(lambda _: VMEM, outs),
        scratch_shapes=list(scratch),
        compiler_params=pltpu.CompilerParams(vmem_limit_bytes=limit),
        cost_estimate=pl.CostEstimate(flops=flops, bytes_accessed=size, transcendentals=0),
    )(*args)


def shape(dims, dtype=BF):
    return jax.ShapeDtypeStruct(dims, dtype)


def per_device(
    normed_input,
    document_index,
    frozen_query_state,
    frozen_keyvalue_weight,
    layer_output_gradient,
    frozen_output_gradient,
    adapter_down_weight,
    query_up_weight,
    keyvalue_up_weight,
    output_down_weight,
    output_up_weight,
):
    x = normed_input[0]
    outgrad = layer_output_gradient[0]
    down = adapter_down_weight.transpose(0, 2, 1).reshape(3 * RANK, WIDTH)
    out_down = output_down_weight.T
    seq = ("x", "y")
    length = lax.axis_size("x") * lax.axis_size("y")
    column = lax.axis_index("y")
    place = jnp.stack([lax.axis_index(seq), column, lax.axis_index("core")]).astype(jnp.int32)

    low, pack = call(
        keyval_kernel, "keyval", (shape((3 * RANK, ROWS)), shape((PACK_ROWS, 2 * KEY_COLUMNS))),
        (x, down, frozen_keyvalue_weight[0], keyvalue_up_weight, document_index),
        flops=10**8, size=2 * 10**6,
    )

    def shifted(array, by):
        return lax.ppermute(array, seq, [(i, (i + by) % length) for i in range(length)])

    blocks = {0: pack}
    for step in range(1, 5):
        blocks[step] = shifted(blocks[step - 1], 1)
        if step < 4:
            blocks[8 - step] = shifted(pack, 7) if step == 1 else shifted(blocks[9 - step], -1)

    q, grad, back_out = call(
        query_kernel, "query",
        (shape((ROWS, QUERY_COLUMNS)), shape((ROWS, QUERY_COLUMNS)), shape((RANK, ROWS))),
        (low, frozen_query_state[0], query_up_weight, outgrad, output_up_weight, frozen_output_gradient[0], out_down),
        flops=10**8, size=4 * 10**6,
    )

    window = SPAN * ROWS
    parts, back_query, low_out, query_term, keyval_term, out_term = call(
        attention_kernel, "attention",
        (
            shape((SPAN, 2 * RANK, ROWS)),
            shape((RANK, ROWS)),
            shape((RANK, ROWS)),
            shape((RANK, QUERY_COLUMNS), F32),
            shape((2 * RANK, KEY_COLUMNS), F32),
            shape((RANK, QUERY_COLUMNS), F32),
        ),
        (place, document_index, low, q, grad, back_out, query_up_weight, keyvalue_up_weight, out_down,
         *[blocks[o] for o in range(SPAN)]),
        scratch=(
            pltpu.VMEM((ROWS, window), F32),
            pltpu.VMEM((window, HEAD_SIZE), BF),
            pltpu.VMEM((window, HEAD_SIZE), BF),
            pltpu.VMEM((RANK, window), BF),
            pltpu.VMEM((RANK, window), BF),
            pltpu.VMEM((2 * RANK, window), F32),
        ),
        flops=4 * 10**9, size=4 * 10**6, smem_first=True,
    )

    parts = lax.all_to_all(parts, "y", 0, 0, tiled=False).astype(F32)
    here = (jnp.arange(SPAN) >= column)[:, None, None]
    kept_back = jnp.sum(jnp.where(here, parts, 0.0), axis=0)
    sent_back = jnp.sum(jnp.where(here, 0.0, parts), axis=0).astype(BF)
    rows_x = lax.axis_size("x")
    there = lax.ppermute(sent_back, "x", [(i, (i - 1) % rows_x) for i in range(rows_x)])

    half = (length, 3 * RANK, ROWS)
    kept, sent = call(
        term_kernel, "terms", (shape(half), shape(half)),
        (place, x, outgrad, back_query, kept_back, there, low_out, query_term, keyval_term, out_term),
        scratch=(pltpu.VMEM((2, *half), BF),),
        flops=10**8, size=4 * 10**6, smem_first=True,
    )

    swap = [(0, 1), (1, 0)]
    total = (kept.astype(F32) + lax.ppermute(sent, "core", swap).astype(F32)).astype(BF)
    total = lax.all_to_all(total, seq, 0, 0, tiled=False)
    total = jnp.sum(total.astype(F32), axis=0).astype(BF)
    depth = lax.axis_size("z")
    total = lax.all_to_all(jnp.broadcast_to(total, (depth, *total.shape)), "z", 0, 0, tiled=False)
    scale = 0.5 / (depth * lax.axis_size("core"))
    total = (jnp.sum(total.astype(F32), axis=0) * scale).astype(BF)
    total = lax.all_to_all(jnp.broadcast_to(total, half), seq, 0, 0, tiled=False)
    other = lax.ppermute(total, "core", swap)

    lora, query_up, keyval_up, output_down, output_up = call(
        unpack_kernel, "unpack",
        (
            shape((3, RANK, WIDTH)),
            shape((RANK, QUERY_COLUMNS)),
            shape((2, RANK, KEY_COLUMNS)),
            shape((RANK, QUERY_COLUMNS)),
            shape((RANK, WIDTH)),
        ),
        (place, total, other),
        scratch=(pltpu.VMEM((2, *half), BF),),
        size=2 * 10**6, smem_first=True,
    )
    return lora.transpose(0, 2, 1), query_up, keyval_up, output_down.T, output_up


def solution(mesh):
    named = Mesh(mesh.devices.reshape(8, 2, 4, 8), ("z", "core", "x", "y"))
    rep, seq = ("z", "core"), ("x", "y")
    split = P(rep, seq, None)
    placed = (split, P(rep, seq), split, split, split, split, P(), P(), P(), P(), P())
    return jax.shard_map(
        per_device, mesh=named, in_specs=placed, out_specs=(P(), P(), P(), P(), P()), check_vma=False
    )
```

```python
import jax
import jax.numpy as jnp
from jax import lax
from jax.experimental import pallas as pl
from jax.experimental.pallas import tpu as pltpu
from jax.sharding import Mesh, PartitionSpec as P

QUERY_HEADS = 16
KEY_HEADS = 4
HEAD_SIZE = 128
KEY_COLUMNS = 512
ROWS = 128
RANK = 16
SPAN = 8
GROUP = QUERY_HEADS // KEY_HEADS
WIDTH = 4096
QUERY_COLUMNS = QUERY_HEADS * HEAD_SIZE
PACK_ROWS = ROWS + 16
BF = jnp.bfloat16
F32 = jnp.float32
INVERSE = 1.0 / HEAD_SIZE**0.5
LOG2E = 1.4426950408889634
DEVICES = 32

NT = (((1,), (1,)), ((), ()))
TN = (((0,), (0,)), ((), ()))
NN = (((1,), (0,)), ((), ()))


def dot(a, b, dims=NN):
    return lax.dot_general(a, b, dims, preferred_element_type=F32)


def keyval_kernel(x_any, down_any, keyval_any, up_any, doc_any, low_ref, pack_ref,
                  x_ref, down_ref, keyval_ref, up_ref, doc_ref, sems):
    pairs = ((x_any, x_ref), (down_any, down_ref), (keyval_any, keyval_ref), (up_any, up_ref), (doc_any, doc_ref))
    copies = [pltpu.make_async_copy(a, b, sems.at[i]) for i, (a, b) in enumerate(pairs)]
    for copy in copies:
        copy.start()
    copies[0].wait()
    copies[1].wait()
    low = dot(down_ref[...], x_ref[...], NT).astype(BF)
    low_ref[...] = low
    for copy in copies[2:]:
        copy.wait()
    for c in range(2):
        part = pl.ds(c * KEY_COLUMNS, KEY_COLUMNS)
        delta = dot(low[(c + 1) * RANK : (c + 2) * RANK], up_ref[c], TN)
        pack_ref[pl.ds(0, ROWS), part] = (
            keyval_ref[:, part].astype(F32) + 0.5 * delta
        ).astype(BF)
    documents = jnp.broadcast_to(doc_ref[...].astype(F32), (RANK, ROWS)).astype(BF)
    pack_ref[pl.ds(ROWS, RANK), :] = jnp.concatenate(
        [low[RANK : 2 * RANK], low[2 * RANK :], documents, jnp.zeros((RANK, 5 * ROWS), BF)], axis=1
    )


def query_kernel(low_ref, query_ref, query_up_ref, outgrad_ref, out_up_ref, frozen_ref, out_down_ref,
                 q_ref, grad_ref, back_out_ref):
    q_ref[...] = (
        query_ref[...].astype(F32) + 0.5 * dot(low_ref[pl.ds(0, RANK), :], query_up_ref[...], TN)
    ).astype(BF)
    back_out = dot(out_up_ref[...], outgrad_ref[...], NT).astype(BF)
    back_out_ref[...] = back_out
    grad_ref[...] = (
        frozen_ref[...].astype(F32) + 0.5 * dot(back_out, out_down_ref[...], TN)
    ).astype(BF)


def attention_kernel(place_ref, doc_ref, low_ref, q_ref, grad_ref, back_out_ref, query_up_ref, up_ref,
                     out_down_ref, *rest):
    blocks = rest[:SPAN]
    parts_ref, back_query_ref, low_out_ref, query_term_ref, keyval_term_ref, out_term_ref = rest[SPAN : SPAN + 6]
    bias, keys, values, low_keys, low_values, back_parts = rest[SPAN + 6 :]
    position = place_ref[0]
    own = jnp.broadcast_to(doc_ref[...].astype(F32), (ROWS, ROWS))
    row = lax.broadcasted_iota(jnp.int32, (ROWS, ROWS), 0)
    col = lax.broadcasted_iota(jnp.int32, (ROWS, ROWS), 1)
    for o in range(SPAN):
        span = pl.ds(o * ROWS, ROWS)
        extra = blocks[o][pl.ds(ROWS, RANK), :]
        low_keys[:, span] = extra[:, :ROWS]
        low_values[:, span] = extra[:, ROWS : 2 * ROWS]
        document = jnp.transpose(jnp.broadcast_to(extra[:1, 2 * ROWS : 3 * ROWS].astype(F32), (ROWS, ROWS)))
        seen = own == document
        if o == 0:
            seen = seen & (row <= col)
        else:
            seen = seen & (jnp.broadcast_to(position, (ROWS, ROWS)) >= o)
        one = jnp.where(seen, 0.0, -1e30)
        for i in range(GROUP):
            bias[span, pl.ds(i*ROWS, ROWS)] = one
    back_parts[...] = jnp.zeros_like(back_parts)
    low_zero = low_ref[pl.ds(0, RANK), :]
    back_out = back_out_ref[...]

    def one_group(g, sums):
        back_query, low_out = sums
        at = pl.ds(pl.multiple_of(g * HEAD_SIZE, HEAD_SIZE), HEAD_SIZE)
        value_at = pl.ds(pl.multiple_of(KEY_COLUMNS + g * HEAD_SIZE, HEAD_SIZE), HEAD_SIZE)
        for o in range(SPAN):
            span = pl.ds(o * ROWS, ROWS)
            keys[span, :] = blocks[o][pl.ds(0, ROWS), at]
            values[span, :] = blocks[o][pl.ds(0, ROWS), value_at]
        heads = [pl.ds(pl.multiple_of((g * GROUP + i) * HEAD_SIZE, HEAD_SIZE), HEAD_SIZE) for i in range(GROUP)]
        q = jnp.concatenate([q_ref[:, h] for h in heads], axis=0)
        grad = jnp.concatenate([grad_ref[:, h] for h in heads], axis=0)
        qT = jnp.transpose(q.astype(F32))
        gradT = jnp.transpose(grad.astype(F32))
        k, v = keys[...], values[...]
        scores = dot(k, qT.astype(BF)) * (INVERSE * LOG2E) + bias[...]
        powers = jnp.exp2(scores - jnp.max(scores, axis=0, keepdims=True))
        recip = 1.0 / jnp.sum(powers, axis=0, keepdims=True)
        powers = powers.astype(BF)
        attn = (dot(v, powers, TN) * recip).astype(BF)
        delta = jnp.sum(gradT * attn.astype(F32), axis=0, keepdims=True)
        dprobs = dot(v, gradT.astype(BF))
        dscores = powers * (dprobs - delta).astype(BF)
        dq = (dot(k, dscores, TN) * (recip * INVERSE)).astype(BF)
        scaled_q = jnp.transpose(qT * (recip * INVERSE)).astype(BF)
        scaled_grad = jnp.transpose(gradT * recip).astype(BF)
        dkeys = dot(dscores, scaled_q).astype(BF)
        dvalues = dot(powers, scaled_grad).astype(BF)
        back_parts[pl.ds(0, RANK), :] += dot(up_ref[0, :, at], dkeys, NT)
        back_parts[pl.ds(RANK, RANK), :] += dot(up_ref[1, :, at], dvalues, NT)
        keyval_term_ref[pl.ds(0, RANK), at] = dot(low_keys[...], dkeys)
        keyval_term_ref[pl.ds(RANK, RANK), at] = dot(low_values[...], dvalues)
        for i, h in enumerate(heads):
            mine = slice(i * ROWS, (i + 1) * ROWS)
            query_term_ref[:, h] = dot(low_zero, dq[:, mine], NT)
            out_term_ref[:, h] = dot(back_out, attn[:, mine], NT)
            back_query = back_query + dot(query_up_ref[:, h], dq[:, mine])
            low_out = low_out + dot(out_down_ref[:, h], attn[:, mine])
        return back_query, low_out

    zero = jnp.zeros((RANK, ROWS), F32)
    back_query, low_out = lax.fori_loop(0, KEY_HEADS, one_group, (zero, zero), unroll=True)
    back_query_ref[...] = back_query.astype(BF)
    low_out_ref[...] = low_out.astype(BF)
    parts_ref[...] = jnp.zeros_like(parts_ref)
    for o in range(SPAN):
        parts_ref[lax.rem(position + (DEVICES - o), DEVICES)] = back_parts[:, pl.ds(o * ROWS, ROWS)].astype(BF)


def term_kernel(place_ref, x_ref, outgrad_ref, back_query_ref, parts_ref, low_out_ref,
                query_term_ref, keyval_term_ref, out_term_ref, kept_ref, sent_ref, both):
    core = place_ref[1]
    back_keyval = parts_ref[0].astype(F32)
    for i in range(1, DEVICES):
        back_keyval = back_keyval + parts_ref[i].astype(F32)
    back_keyval = back_keyval.astype(BF)
    back = jnp.concatenate([back_query_ref[...], back_keyval], axis=0)
    down = dot(back, x_ref[...]).astype(BF)
    up = dot(low_out_ref[...], outgrad_ref[...]).astype(BF)
    query_term = query_term_ref[...].astype(BF)
    keyval_term = keyval_term_ref[...].astype(BF)
    out_term = out_term_ref[...].astype(BF)

    def put(half, tile, value):
        both[half, tile // 3, pl.ds(tile % 3 * RANK, RANK), :] = value

    def tiles(half, first, array):
        for t in range(array.shape[1] // ROWS):
            put(half, first + t, array[:, t * ROWS : (t + 1) * ROWS])
        return first + array.shape[1] // ROWS

    first = 0
    for c in range(3):
        first = tiles(0, first, down[c * RANK : (c + 1) * RANK])
    first = tiles(1, 0, query_term)
    first = tiles(1, first, keyval_term[:RANK])
    first = tiles(1, first, keyval_term[RANK:])
    first = tiles(1, first, out_term)
    first = tiles(1, first, up)
    for t in range(first, 96):
        put(1, t, jnp.zeros((RANK, ROWS), BF))
    kept_ref[...] = both[core]
    sent_ref[...] = both[1 - core]


def unpack_kernel(place_ref, kept_ref, sent_ref, down_ref, query_ref, keyval_ref, out_down_ref, out_up_ref, both):
    core = place_ref[1]
    both[core] = kept_ref[...]
    both[1 - core] = sent_ref[...]

    def get(half, tile):
        return both[half, tile // 3, pl.ds(tile % 3 * RANK, RANK), :]

    for c in range(3):
        for t in range(WIDTH // ROWS):
            down_ref[c, :, pl.ds(t * ROWS, ROWS)] = get(0, c * (WIDTH // ROWS) + t)
    first = 0
    for ref, lead in ((query_ref, None), (keyval_ref, 0), (keyval_ref, 1), (out_down_ref, None), (out_up_ref, None)):
        count = ref.shape[-1] // ROWS
        for t in range(count):
            if lead is None:
                ref[:, pl.ds(t * ROWS, ROWS)] = get(1, first + t)
            else:
                ref[lead, :, pl.ds(t * ROWS, ROWS)] = get(1, first + t)
        first += count


VMEM = pl.BlockSpec(memory_space=pltpu.VMEM)
SMEM = pl.BlockSpec(memory_space=pltpu.SMEM)


def call(kernel, name, outs, args, scratch=(), flops=0, size=0, smem_first=False, limit=32 << 20, kind=None):
    specs = [SMEM if smem_first and i == 0 else (kind or VMEM) for i in range(len(args))]
    return pl.pallas_call(
        kernel,
        name=name,
        out_shape=outs,
        in_specs=specs,
        out_specs=jax.tree.map(lambda _: VMEM, outs),
        scratch_shapes=list(scratch),
        compiler_params=pltpu.CompilerParams(vmem_limit_bytes=limit),
        cost_estimate=pl.CostEstimate(flops=flops, bytes_accessed=size, transcendentals=0),
    )(*args)


def shape(dims, dtype=BF):
    return jax.ShapeDtypeStruct(dims, dtype)


def per_device(
    normed_input,
    document_index,
    frozen_query_state,
    frozen_keyvalue_weight,
    layer_output_gradient,
    frozen_output_gradient,
    adapter_down_weight,
    query_up_weight,
    keyvalue_up_weight,
    output_down_weight,
    output_up_weight,
):
    x = normed_input[0]
    outgrad = layer_output_gradient[0]
    down = adapter_down_weight.transpose(0, 2, 1).reshape(3 * RANK, WIDTH)
    out_down = output_down_weight.T
    seq = ("x", "y")
    length = lax.axis_size("x") * lax.axis_size("y")
    place = jnp.stack([lax.axis_index(seq), lax.axis_index("core")]).astype(jnp.int32)

    low, pack = call(
        keyval_kernel, "keyval", (shape((3 * RANK, ROWS)), shape((PACK_ROWS, 2 * KEY_COLUMNS))),
        (x, down, frozen_keyvalue_weight[0], keyvalue_up_weight, document_index),
        scratch=(
            pltpu.VMEM((ROWS, WIDTH), BF),
            pltpu.VMEM((3 * RANK, WIDTH), BF),
            pltpu.VMEM((ROWS, 2 * KEY_COLUMNS), BF),
            pltpu.VMEM((2, RANK, KEY_COLUMNS), BF),
            pltpu.VMEM((1, ROWS), jnp.int32),
            pltpu.SemaphoreType.DMA((5,)),
        ),
        flops=10**8, size=2 * 10**6, limit=56 << 20, kind=pl.BlockSpec(memory_space=pl.ANY),
    )

    def shifted(array, by):
        return lax.ppermute(array, seq, [(i, (i + by) % length) for i in range(length)])

    blocks = {0: pack}
    for step in range(1, 4):
        blocks[step] = shifted(blocks[step - 1], 1)
        blocks[8 - step] = shifted(pack, 7) if step == 1 else shifted(blocks[9 - step], -1)
    blocks[4] = shifted(blocks[2], 2)

    q, grad, back_out = call(
        query_kernel, "query",
        (shape((ROWS, QUERY_COLUMNS)), shape((ROWS, QUERY_COLUMNS)), shape((RANK, ROWS))),
        (low, frozen_query_state[0], query_up_weight, outgrad, output_up_weight, frozen_output_gradient[0], out_down),
        flops=10**8, size=4 * 10**6,
    )

    window = SPAN * ROWS
    parts, back_query, low_out, query_term, keyval_term, out_term = call(
        attention_kernel, "attention",
        (
            shape((DEVICES, 2 * RANK, ROWS)),
            shape((RANK, ROWS)),
            shape((RANK, ROWS)),
            shape((RANK, QUERY_COLUMNS), F32),
            shape((2 * RANK, KEY_COLUMNS), F32),
            shape((RANK, QUERY_COLUMNS), F32),
        ),
        (place, document_index, low, q, grad, back_out, query_up_weight, keyvalue_up_weight, out_down,
         *[blocks[o] for o in range(SPAN)]),
        scratch=(
            pltpu.VMEM((window, GROUP * ROWS), F32),
            pltpu.VMEM((window, HEAD_SIZE), BF),
            pltpu.VMEM((window, HEAD_SIZE), BF),
            pltpu.VMEM((RANK, window), BF),
            pltpu.VMEM((RANK, window), BF),
            pltpu.VMEM((2 * RANK, window), F32),
        ),
        flops=4 * 10**9, size=4 * 10**6, smem_first=True,
    )

    parts = lax.all_to_all(parts, seq, 0, 0, tiled=False)

    half = (length, 3 * RANK, ROWS)
    kept, sent = call(
        term_kernel, "terms", (shape(half), shape(half)),
        (place, x, outgrad, back_query, parts, low_out, query_term, keyval_term, out_term),
        scratch=(pltpu.VMEM((2, *half), BF),),
        flops=10**8, size=4 * 10**6, smem_first=True,
    )

    swap = [(0, 1), (1, 0)]
    total = (kept.astype(F32) + lax.ppermute(sent, "core", swap).astype(F32)).astype(BF)
    total = lax.all_to_all(total, seq, 0, 0, tiled=False)
    total = jnp.sum(total.astype(F32), axis=0).astype(BF)
    depth = lax.axis_size("z")
    total = lax.all_to_all(jnp.broadcast_to(total, (depth, *total.shape)), "z", 0, 0, tiled=False)
    scale = 0.5 / (depth * lax.axis_size("core"))
    total = (jnp.sum(total.astype(F32), axis=0) * scale).astype(BF)
    total = lax.all_to_all(jnp.broadcast_to(total, half), seq, 0, 0, tiled=False)
    other = lax.ppermute(total, "core", swap)

    lora, query_up, keyval_up, output_down, output_up = call(
        unpack_kernel, "unpack",
        (
            shape((3, RANK, WIDTH)),
            shape((RANK, QUERY_COLUMNS)),
            shape((2, RANK, KEY_COLUMNS)),
            shape((RANK, QUERY_COLUMNS)),
            shape((RANK, WIDTH)),
        ),
        (place, total, other),
        scratch=(pltpu.VMEM((2, *half), BF),),
        size=2 * 10**6, smem_first=True,
    )
    return lora.transpose(0, 2, 1), query_up, keyval_up, output_down.T, output_up


def solution(mesh):
    named = Mesh(mesh.devices.reshape(8, 2, 4, 8), ("z", "core", "x", "y"))
    rep, seq = ("z", "core"), ("x", "y")
    split = P(rep, seq, None)
    placed = (split, P(rep, seq), split, split, split, split, P(), P(), P(), P(), P())
    return jax.shard_map(
        per_device, mesh=named, in_specs=placed, out_specs=(P(), P(), P(), P(), P()), check_vma=False
    )
```

```python
import jax
import jax.numpy as jnp
from jax import lax
from jax.experimental import pallas as pl
from jax.experimental.pallas import tpu as pltpu
from jax.sharding import Mesh, PartitionSpec as P

QUERY_HEADS = 16
KEY_HEADS = 4
HEAD_SIZE = 128
KEY_COLUMNS = 512
ROWS = 128
RANK = 16
SPAN = 8
GROUP = QUERY_HEADS // KEY_HEADS
WIDTH = 4096
QUERY_COLUMNS = QUERY_HEADS * HEAD_SIZE
PACK_ROWS = ROWS + 16
BF = jnp.bfloat16
F32 = jnp.float32
INVERSE = 1.0 / HEAD_SIZE**0.5
DEVICES = 32
LOG2E = 1.4426950408889634

NT = (((1,), (1,)), ((), ()))
TN = (((0,), (0,)), ((), ()))
NN = (((1,), (0,)), ((), ()))


def dot(a, b, dims=NN):
    return lax.dot_general(a, b, dims, preferred_element_type=F32)


def keyval_kernel(x_any, down_any, keyval_any, up_any, doc_any, low_ref, pack_ref,
                  x_ref, down_ref, keyval_ref, up_ref, doc_ref, sems):
    pairs = ((x_any, x_ref), (down_any, down_ref), (keyval_any, keyval_ref), (up_any, up_ref), (doc_any, doc_ref))
    copies = [pltpu.make_async_copy(a, b, sems.at[i]) for i, (a, b) in enumerate(pairs)]
    for copy in copies:
        copy.start()
    copies[0].wait()
    copies[1].wait()
    low = dot(down_ref[...], x_ref[...], NT).astype(BF)
    low_ref[...] = low
    for copy in copies[2:]:
        copy.wait()
    for c in range(2):
        part = pl.ds(c * KEY_COLUMNS, KEY_COLUMNS)
        delta = dot(low[(c + 1) * RANK : (c + 2) * RANK], up_ref[c], TN)
        pack_ref[pl.ds(0, ROWS), part] = (
            keyval_ref[:, part].astype(F32) + 0.5 * delta
        ).astype(BF)
    documents = jnp.broadcast_to(doc_ref[...].astype(F32), (RANK, ROWS)).astype(BF)
    pack_ref[pl.ds(ROWS, RANK), :] = jnp.concatenate(
        [low[RANK : 2 * RANK], low[2 * RANK :], documents, jnp.zeros((RANK, 5 * ROWS), BF)], axis=1
    )


def query_kernel(low_any, query_any, query_up_any, outgrad_any, out_up_any, frozen_any, out_down_any,
                 q_ref, grad_ref, back_out_ref,
                 low_ref, query_ref, query_up_ref, outgrad_ref, out_up_ref, frozen_ref, out_down_ref, sems):
    pairs = ((outgrad_any, outgrad_ref), (out_up_any, out_up_ref), (low_any, low_ref), (query_up_any, query_up_ref),
             (query_any, query_ref), (out_down_any, out_down_ref), (frozen_any, frozen_ref))
    copies = [pltpu.make_async_copy(a, b, sems.at[i]) for i, (a, b) in enumerate(pairs)]
    for copy in copies:
        copy.start()
    for copy in copies[:5]:
        copy.wait()
    back_out = dot(out_up_ref[...], outgrad_ref[...], NT).astype(BF)
    back_out_ref[...] = back_out
    q_ref[...] = (
        query_ref[...].astype(F32) + 0.5 * dot(low_ref[pl.ds(0, RANK), :], query_up_ref[...], TN)
    ).astype(BF)
    for copy in copies[5:]:
        copy.wait()
    grad_ref[...] = (
        frozen_ref[...].astype(F32) + 0.5 * dot(back_out, out_down_ref[...], TN)
    ).astype(BF)


def attention_kernel(low_ref, q_ref, grad_ref, back_out_ref, query_up_ref, up_ref,
                     out_down_ref, *rest):
    blocks = rest[:SPAN]
    parts_ref, back_query_ref, low_out_ref, query_term_ref, keyval_term_ref, out_term_ref = rest[SPAN : SPAN + 6]
    bias, keys, values, low_keys, low_values, back_parts = rest[SPAN + 6 :]
    position = lax.axis_index("x") * SPAN + lax.axis_index("y")
    own = blocks[0][pl.ds(ROWS, RANK), pl.ds(2 * ROWS, ROWS)][:1]
    own = jnp.broadcast_to(own.astype(F32), (ROWS, ROWS))
    row = lax.broadcasted_iota(jnp.int32, (ROWS, ROWS), 0)
    col = lax.broadcasted_iota(jnp.int32, (ROWS, ROWS), 1)
    for o in range(SPAN):
        span = pl.ds(o * ROWS, ROWS)
        extra = blocks[o][pl.ds(ROWS, RANK), :]
        low_keys[:, span] = extra[:, :ROWS]
        low_values[:, span] = extra[:, ROWS : 2 * ROWS]
        document = jnp.transpose(jnp.broadcast_to(extra[:1, 2 * ROWS : 3 * ROWS].astype(F32), (ROWS, ROWS)))
        seen = own == document
        if o == 0:
            seen = seen & (row <= col)
        else:
            seen = seen & (jnp.broadcast_to(position, (ROWS, ROWS)) >= o)
        one = jnp.where(seen, 0.0, -1e30)
        for i in range(GROUP):
            bias[span, pl.ds(i*ROWS, ROWS)] = one
    back_parts[...] = jnp.zeros_like(back_parts)
    low_zero = low_ref[pl.ds(0, RANK), :]
    back_out = back_out_ref[...]

    def one_group(g, sums):
        back_query, low_out = sums
        at = pl.ds(pl.multiple_of(g * HEAD_SIZE, HEAD_SIZE), HEAD_SIZE)
        value_at = pl.ds(pl.multiple_of(KEY_COLUMNS + g * HEAD_SIZE, HEAD_SIZE), HEAD_SIZE)
        for o in range(SPAN):
            span = pl.ds(o * ROWS, ROWS)
            keys[span, :] = blocks[o][pl.ds(0, ROWS), at]
            values[span, :] = blocks[o][pl.ds(0, ROWS), value_at]
        heads = [pl.ds(pl.multiple_of((g * GROUP + i) * HEAD_SIZE, HEAD_SIZE), HEAD_SIZE) for i in range(GROUP)]
        q = jnp.concatenate([q_ref[:, h] for h in heads], axis=0)
        grad = jnp.concatenate([grad_ref[:, h] for h in heads], axis=0)
        qT = jnp.transpose(q.astype(F32))
        gradT = jnp.transpose(grad.astype(F32))
        k, v = keys[...], values[...]
        scores = dot(k, qT.astype(BF)) * (INVERSE * LOG2E) + bias[...]
        powers = jnp.exp2(scores - jnp.max(scores, axis=0, keepdims=True))
        recip = 1.0 / jnp.sum(powers, axis=0, keepdims=True)
        powers = powers.astype(BF)
        attn = (dot(v, powers, TN) * recip).astype(BF)
        delta = jnp.sum(gradT * attn.astype(F32), axis=0, keepdims=True)
        dprobs = dot(v, gradT.astype(BF))
        dscores = powers * (dprobs - delta).astype(BF)
        dq = (dot(k, dscores, TN) * (recip * INVERSE)).astype(BF)
        scaled_q = jnp.transpose(qT * (recip * INVERSE)).astype(BF)
        scaled_grad = jnp.transpose(gradT * recip).astype(BF)
        dkeys = dot(dscores, scaled_q).astype(BF)
        dvalues = dot(powers, scaled_grad).astype(BF)
        back_parts[pl.ds(0, RANK), :] += dot(up_ref[0, :, at], dkeys, NT)
        back_parts[pl.ds(RANK, RANK), :] += dot(up_ref[1, :, at], dvalues, NT)
        keyval_term_ref[pl.ds(0, RANK), at] = dot(low_keys[...], dkeys)
        keyval_term_ref[pl.ds(RANK, RANK), at] = dot(low_values[...], dvalues)
        for i, h in enumerate(heads):
            mine = slice(i * ROWS, (i + 1) * ROWS)
            query_term_ref[:, h] = dot(low_zero, dq[:, mine], NT)
            out_term_ref[:, h] = dot(back_out, attn[:, mine], NT)
            back_query = back_query + dot(query_up_ref[:, h], dq[:, mine])
            low_out = low_out + dot(out_down_ref[:, h], attn[:, mine])
        return back_query, low_out

    zero = jnp.zeros((RANK, ROWS), F32)
    back_query, low_out = lax.fori_loop(0, KEY_HEADS, one_group, (zero, zero), unroll=True)
    back_query_ref[...] = back_query.astype(BF)
    low_out_ref[...] = low_out.astype(BF)
    parts_ref[...] = jnp.zeros_like(parts_ref)
    for o in range(SPAN):
        parts_ref[lax.rem(position + (DEVICES - o), DEVICES)] = back_parts[:, pl.ds(o * ROWS, ROWS)].astype(BF)


def term_kernel(x_ref, outgrad_ref, back_query_ref, parts_ref, low_out_ref,
                query_term_ref, keyval_term_ref, out_term_ref, kept_ref, sent_ref, both):
    core = lax.axis_index("core")
    back_keyval = parts_ref[0].astype(F32)
    for i in range(1, DEVICES):
        back_keyval = back_keyval + parts_ref[i].astype(F32)
    back = jnp.concatenate([back_query_ref[...], back_keyval.astype(BF)], axis=0)
    down = dot(back, x_ref[...]).astype(BF)
    up = dot(low_out_ref[...], outgrad_ref[...]).astype(BF)
    query_term = query_term_ref[...].astype(BF)
    keyval_term = keyval_term_ref[...].astype(BF)
    out_term = out_term_ref[...].astype(BF)

    def put(half, tile, value):
        both[half, tile // 3, pl.ds(tile % 3 * RANK, RANK), :] = value

    def tiles(half, first, array):
        for t in range(array.shape[1] // ROWS):
            put(half, first + t, array[:, t * ROWS : (t + 1) * ROWS])
        return first + array.shape[1] // ROWS

    first = 0
    for c in range(3):
        first = tiles(0, first, down[c * RANK : (c + 1) * RANK])
    first = tiles(1, 0, query_term)
    first = tiles(1, first, keyval_term[:RANK])
    first = tiles(1, first, keyval_term[RANK:])
    first = tiles(1, first, out_term)
    first = tiles(1, first, up)
    for t in range(first, 96):
        put(1, t, jnp.zeros((RANK, ROWS), BF))
    kept_ref[...] = both[core]
    sent_ref[...] = both[1 - core]


def unpack_kernel(kept_ref, sent_ref, down_ref, query_ref, keyval_ref, out_down_ref, out_up_ref, both):
    core = lax.axis_index("core")
    both[core] = kept_ref[...]
    both[1 - core] = sent_ref[...]

    def get(half, tile):
        return both[half, tile // 3, pl.ds(tile % 3 * RANK, RANK), :]

    for c in range(3):
        for t in range(WIDTH // ROWS):
            down_ref[c, :, pl.ds(t * ROWS, ROWS)] = get(0, c * (WIDTH // ROWS) + t)
    first = 0
    for ref, lead in ((query_ref, None), (keyval_ref, 0), (keyval_ref, 1), (out_down_ref, None), (out_up_ref, None)):
        count = ref.shape[-1] // ROWS
        for t in range(count):
            if lead is None:
                ref[:, pl.ds(t * ROWS, ROWS)] = get(1, first + t)
            else:
                ref[lead, :, pl.ds(t * ROWS, ROWS)] = get(1, first + t)
        first += count


VMEM = pl.BlockSpec(memory_space=pltpu.VMEM)


def call(kernel, name, outs, args, scratch=(), flops=0, size=0, limit=32 << 20, kind=None):
    specs = [kind or VMEM] * len(args)
    return pl.pallas_call(
        kernel,
        name=name,
        out_shape=outs,
        in_specs=specs,
        out_specs=jax.tree.map(lambda _: VMEM, outs),
        scratch_shapes=list(scratch),
        compiler_params=pltpu.CompilerParams(vmem_limit_bytes=limit),
        cost_estimate=pl.CostEstimate(flops=flops, bytes_accessed=size, transcendentals=0),
    )(*args)


def shape(dims, dtype=BF):
    return jax.ShapeDtypeStruct(dims, dtype)


def chain_pairs(length):
    up = [[(i, i + 1) for i in range(step, length - 1)] for step in range(SPAN // 2)]
    down, wanted = [], {(place - 5, place) for place in range(5, length)}
    for _ in range(2):
        down.insert(0, sorted(((place + 1) % length, place) for _, place in wanted))
        earlier = {(block, (place + 1) % length) for block, place in wanted}
        offset = 5 + len(down)
        wanted = earlier | {(place - offset, place) for place in range(offset, length)}
    down.insert(0, sorted(wanted))
    return up, down


def per_device(
    normed_input,
    document_index,
    frozen_query_state,
    frozen_keyvalue_weight,
    layer_output_gradient,
    frozen_output_gradient,
    adapter_down_weight,
    query_up_weight,
    keyvalue_up_weight,
    output_down_weight,
    output_up_weight,
):
    x = normed_input[0]
    outgrad = layer_output_gradient[0]
    down = adapter_down_weight.transpose(0, 2, 1).reshape(3 * RANK, WIDTH)
    out_down = output_down_weight.T
    seq = ("x", "y")
    length = lax.axis_size("x") * lax.axis_size("y")

    low, pack = call(
        keyval_kernel, "keyval", (shape((3 * RANK, ROWS)), shape((PACK_ROWS, 2 * KEY_COLUMNS))),
        (x, down, frozen_keyvalue_weight[0], keyvalue_up_weight, document_index),
        scratch=(
            pltpu.VMEM((ROWS, WIDTH), BF),
            pltpu.VMEM((3 * RANK, WIDTH), BF),
            pltpu.VMEM((ROWS, 2 * KEY_COLUMNS), BF),
            pltpu.VMEM((2, RANK, KEY_COLUMNS), BF),
            pltpu.VMEM((1, ROWS), jnp.int32),
            pltpu.SemaphoreType.DMA((5,)),
        ),
        flops=10**8, size=2 * 10**6, limit=56 << 20, kind=pl.BlockSpec(memory_space=pl.ANY),
    )

    blocks = {0: pack}
    up, down = chain_pairs(length)
    for step in range(1, 3):
        blocks[step] = lax.ppermute(blocks[step - 1], seq, up[step - 1])
        blocks[8 - step] = lax.ppermute(blocks[(9 - step) % SPAN], seq, down[step - 1])

    q, grad, back_out = call(
        query_kernel, "query",
        (shape((ROWS, QUERY_COLUMNS)), shape((ROWS, QUERY_COLUMNS)), shape((RANK, ROWS))),
        (low, frozen_query_state[0], query_up_weight, outgrad, output_up_weight, frozen_output_gradient[0], out_down),
        scratch=(
            pltpu.VMEM((3 * RANK, ROWS), BF),
            pltpu.VMEM((ROWS, QUERY_COLUMNS), BF),
            pltpu.VMEM((RANK, QUERY_COLUMNS), BF),
            pltpu.VMEM((ROWS, WIDTH), BF),
            pltpu.VMEM((RANK, WIDTH), BF),
            pltpu.VMEM((ROWS, QUERY_COLUMNS), BF),
            pltpu.VMEM((RANK, QUERY_COLUMNS), BF),
            pltpu.SemaphoreType.DMA((7,)),
        ),
        flops=10**8, size=4 * 10**6, limit=56 << 20, kind=pl.BlockSpec(memory_space=pl.ANY),
    )

    blocks[2], _ = lax.optimization_barrier((blocks[2], back_out))
    blocks[3] = lax.ppermute(blocks[2], seq, up[2])
    blocks[5] = lax.ppermute(blocks[6], seq, down[2])
    blocks[4] = lax.ppermute(blocks[3], seq, up[3])

    window = SPAN * ROWS
    parts, back_query, low_out, query_term, keyval_term, out_term = call(
        attention_kernel, "attention",
        (
            shape((DEVICES, 2 * RANK, ROWS)),
            shape((RANK, ROWS)),
            shape((RANK, ROWS)),
            shape((RANK, QUERY_COLUMNS), F32),
            shape((2 * RANK, KEY_COLUMNS), F32),
            shape((RANK, QUERY_COLUMNS), F32),
        ),
        (low, q, grad, back_out, query_up_weight, keyvalue_up_weight, out_down,
         *[blocks[o] for o in range(SPAN)]),
        scratch=(
            pltpu.VMEM((window, GROUP * ROWS), F32),
            pltpu.VMEM((window, HEAD_SIZE), BF),
            pltpu.VMEM((window, HEAD_SIZE), BF),
            pltpu.VMEM((RANK, window), BF),
            pltpu.VMEM((RANK, window), BF),
            pltpu.VMEM((2 * RANK, window), F32),
        ),
        flops=4 * 10**9, size=4 * 10**6,
    )

    parts = lax.all_to_all(parts, seq, 0, 0, tiled=False)

    half = (length, 3 * RANK, ROWS)
    kept, sent = call(
        term_kernel, "terms", (shape(half), shape(half)),
        (x, outgrad, back_query, parts, low_out, query_term, keyval_term, out_term),
        scratch=(pltpu.VMEM((2, *half), BF),),
        flops=10**8, size=4 * 10**6,
    )

    swap = [(0, 1), (1, 0)]
    total = (kept.astype(F32) + lax.ppermute(sent, "core", swap).astype(F32)).astype(BF)
    total = lax.all_to_all(total, seq, 0, 0, tiled=False)
    total = jnp.sum(total.astype(F32), axis=0).astype(BF)
    depth = lax.axis_size("z")
    total = lax.all_to_all(jnp.broadcast_to(total, (depth, *total.shape)), "z", 0, 0, tiled=False)
    scale = 0.5 / (depth * lax.axis_size("core"))
    total = (jnp.sum(total.astype(F32), axis=0) * scale).astype(BF)
    total = lax.all_to_all(jnp.broadcast_to(total, half), seq, 0, 0, tiled=False)
    other = lax.ppermute(total, "core", swap)

    lora, query_up, keyval_up, output_down, output_up = call(
        unpack_kernel, "unpack",
        (
            shape((3, RANK, WIDTH)),
            shape((RANK, QUERY_COLUMNS)),
            shape((2, RANK, KEY_COLUMNS)),
            shape((RANK, QUERY_COLUMNS)),
            shape((RANK, WIDTH)),
        ),
        (total, other),
        scratch=(pltpu.VMEM((2, *half), BF),),
        size=2 * 10**6,
    )
    return lora.transpose(0, 2, 1), query_up, keyval_up, output_down.T, output_up


def solution(mesh):
    named = Mesh(mesh.devices.reshape(8, 2, 4, 8), ("z", "core", "x", "y"))
    rep, seq = ("z", "core"), ("x", "y")
    split = P(rep, seq, None)
    placed = (split, P(rep, seq), split, split, split, split, P(), P(), P(), P(), P())
    return jax.shard_map(
        per_device, mesh=named, in_specs=placed, out_specs=(P(), P(), P(), P(), P()), check_vma=False
    )
```

```python
import jax
import jax.numpy as jnp
from jax import lax
from jax.experimental import pallas as pl
from jax.experimental.pallas import tpu as pltpu
from jax.sharding import Mesh, PartitionSpec as P

QUERY_HEADS = 16
KEY_HEADS = 4
HEAD_SIZE = 128
KEY_COLUMNS = 512
ROWS = 128
RANK = 16
SPAN = 8
GROUP = QUERY_HEADS // KEY_HEADS
WIDTH = 4096
QUERY_COLUMNS = QUERY_HEADS * HEAD_SIZE
PACK_ROWS = ROWS + 16
BF = jnp.bfloat16
F32 = jnp.float32
INVERSE = 1.0 / HEAD_SIZE**0.5
DEVICES = 32
LOG2E = 1.4426950408889634

NT = (((1,), (1,)), ((), ()))
TN = (((0,), (0,)), ((), ()))
NN = (((1,), (0,)), ((), ()))


def dot(a, b, dims=NN):
    return lax.dot_general(a, b, dims, preferred_element_type=F32)


def keyval_kernel(x_any, down_any, keyval_any, up_any, doc_any, low_ref, pack_ref,
                  x_ref, down_ref, keyval_ref, up_ref, doc_ref, sems):
    pairs = ((x_any, x_ref), (down_any, down_ref), (keyval_any, keyval_ref), (up_any, up_ref), (doc_any, doc_ref))
    copies = [pltpu.make_async_copy(a, b, sems.at[i]) for i, (a, b) in enumerate(pairs)]
    for copy in copies:
        copy.start()
    copies[0].wait()
    copies[1].wait()
    low = dot(down_ref[...], x_ref[...], NT).astype(BF)
    low_ref[...] = low
    for copy in copies[2:]:
        copy.wait()
    for c in range(2):
        part = pl.ds(c * KEY_COLUMNS, KEY_COLUMNS)
        delta = dot(low[(c + 1) * RANK : (c + 2) * RANK], up_ref[c], TN)
        pack_ref[pl.ds(0, ROWS), part] = (
            keyval_ref[:, part].astype(F32) + 0.5 * delta
        ).astype(BF)
    documents = jnp.broadcast_to(doc_ref[...].astype(F32), (RANK, ROWS)).astype(BF)
    pack_ref[pl.ds(ROWS, RANK), :] = jnp.concatenate(
        [low[RANK : 2 * RANK], low[2 * RANK :], documents, jnp.zeros((RANK, 5 * ROWS), BF)], axis=1
    )


def query_kernel(low_ref, query_ref, query_up_ref, outgrad_ref, out_up_ref, frozen_ref, out_down_ref,
                 q_ref, grad_ref, back_out_ref):
    q_ref[...] = (
        query_ref[...].astype(F32) + 0.5 * dot(low_ref[pl.ds(0, RANK), :], query_up_ref[...], TN)
    ).astype(BF)
    back_out = dot(out_up_ref[...], outgrad_ref[...], NT).astype(BF)
    back_out_ref[...] = back_out
    grad_ref[...] = (
        frozen_ref[...].astype(F32) + 0.5 * dot(back_out, out_down_ref[...], TN)
    ).astype(BF)


def attention_kernel(low_ref, q_ref, grad_ref, back_out_ref, query_up_ref, up_ref,
                     out_down_ref, *rest):
    blocks = rest[:SPAN]
    parts_ref, back_query_ref, low_out_ref, query_term_ref, keyval_term_ref, out_term_ref = rest[SPAN : SPAN + 6]
    bias, keys, values, low_keys, low_values, back_parts = rest[SPAN + 6 :]
    position = lax.axis_index("x") * SPAN + lax.axis_index("y")
    own = blocks[0][pl.ds(ROWS, RANK), pl.ds(2 * ROWS, ROWS)][:1]
    own = jnp.broadcast_to(own.astype(F32), (ROWS, ROWS))
    row = lax.broadcasted_iota(jnp.int32, (ROWS, ROWS), 0)
    col = lax.broadcasted_iota(jnp.int32, (ROWS, ROWS), 1)
    for o in range(SPAN):
        span = pl.ds(o * ROWS, ROWS)
        extra = blocks[o][pl.ds(ROWS, RANK), :]
        low_keys[:, span] = extra[:, :ROWS]
        low_values[:, span] = extra[:, ROWS : 2 * ROWS]
        document = jnp.transpose(jnp.broadcast_to(extra[:1, 2 * ROWS : 3 * ROWS].astype(F32), (ROWS, ROWS)))
        seen = own == document
        if o == 0:
            seen = seen & (row <= col)
        else:
            seen = seen & (jnp.broadcast_to(position, (ROWS, ROWS)) >= o)
        one = jnp.where(seen, 0.0, -1e30)
        for i in range(GROUP):
            bias[span, pl.ds(i*ROWS, ROWS)] = one
    back_parts[...] = jnp.zeros_like(back_parts)
    low_zero = low_ref[pl.ds(0, RANK), :]
    back_out = back_out_ref[...]

    def one_group(g, sums):
        back_query, low_out = sums
        at = pl.ds(pl.multiple_of(g * HEAD_SIZE, HEAD_SIZE), HEAD_SIZE)
        value_at = pl.ds(pl.multiple_of(KEY_COLUMNS + g * HEAD_SIZE, HEAD_SIZE), HEAD_SIZE)
        for o in range(SPAN):
            span = pl.ds(o * ROWS, ROWS)
            keys[span, :] = blocks[o][pl.ds(0, ROWS), at]
            values[span, :] = blocks[o][pl.ds(0, ROWS), value_at]
        heads = [pl.ds(pl.multiple_of((g * GROUP + i) * HEAD_SIZE, HEAD_SIZE), HEAD_SIZE) for i in range(GROUP)]
        q = jnp.concatenate([q_ref[:, h] for h in heads], axis=0)
        grad = jnp.concatenate([grad_ref[:, h] for h in heads], axis=0)
        qT = jnp.transpose(q.astype(F32))
        gradT = jnp.transpose(grad.astype(F32))
        k, v = keys[...], values[...]
        scores = dot(k, qT.astype(BF)) * (INVERSE * LOG2E) + bias[...]
        powers = jnp.exp2(scores - jnp.max(scores, axis=0, keepdims=True))
        recip = 1.0 / jnp.sum(powers, axis=0, keepdims=True)
        powers = powers.astype(BF)
        attn = (dot(v, powers, TN) * recip).astype(BF)
        delta = jnp.sum(gradT * attn.astype(F32), axis=0, keepdims=True)
        dprobs = dot(v, gradT.astype(BF))
        dscores = powers * (dprobs - delta).astype(BF)
        dq = (dot(k, dscores, TN) * (recip * INVERSE)).astype(BF)
        scaled_q = jnp.transpose(qT * (recip * INVERSE)).astype(BF)
        scaled_grad = jnp.transpose(gradT * recip).astype(BF)
        dkeys = dot(dscores, scaled_q).astype(BF)
        dvalues = dot(powers, scaled_grad).astype(BF)
        back_parts[pl.ds(0, RANK), :] += dot(up_ref[0, :, at], dkeys, NT)
        back_parts[pl.ds(RANK, RANK), :] += dot(up_ref[1, :, at], dvalues, NT)
        keyval_term_ref[pl.ds(0, RANK), at] = dot(low_keys[...], dkeys)
        keyval_term_ref[pl.ds(RANK, RANK), at] = dot(low_values[...], dvalues)
        for i, h in enumerate(heads):
            mine = slice(i * ROWS, (i + 1) * ROWS)
            query_term_ref[:, h] = dot(low_zero, dq[:, mine], NT)
            out_term_ref[:, h] = dot(back_out, attn[:, mine], NT)
            back_query = back_query + dot(query_up_ref[:, h], dq[:, mine])
            low_out = low_out + dot(out_down_ref[:, h], attn[:, mine])
        return back_query, low_out

    zero = jnp.zeros((RANK, ROWS), F32)
    back_query, low_out = lax.fori_loop(0, KEY_HEADS, one_group, (zero, zero), unroll=True)
    back_query_ref[...] = back_query.astype(BF)
    low_out_ref[...] = low_out.astype(BF)
    parts_ref[...] = jnp.zeros_like(parts_ref)
    for o in range(SPAN):
        parts_ref[lax.rem(position + (DEVICES - o), DEVICES)] = back_parts[:, pl.ds(o * ROWS, ROWS)].astype(BF)


def term_kernel(x_ref, outgrad_ref, back_query_ref, parts_ref, low_out_ref,
                query_term_ref, keyval_term_ref, out_term_ref, kept_ref, sent_ref, both):
    core = lax.axis_index("core")
    back_keyval = parts_ref[0].astype(F32)
    for i in range(1, DEVICES):
        back_keyval = back_keyval + parts_ref[i].astype(F32)
    back = jnp.concatenate([back_query_ref[...], back_keyval.astype(BF)], axis=0)
    down = dot(back, x_ref[...]).astype(BF)
    up = dot(low_out_ref[...], outgrad_ref[...]).astype(BF)
    query_term = query_term_ref[...].astype(BF)
    keyval_term = keyval_term_ref[...].astype(BF)
    out_term = out_term_ref[...].astype(BF)

    def put(half, tile, value):
        both[half, tile // 3, pl.ds(tile % 3 * RANK, RANK), :] = value

    def tiles(half, first, array):
        for t in range(array.shape[1] // ROWS):
            put(half, first + t, array[:, t * ROWS : (t + 1) * ROWS])
        return first + array.shape[1] // ROWS

    first = 0
    for c in range(3):
        first = tiles(0, first, down[c * RANK : (c + 1) * RANK])
    first = tiles(1, 0, query_term)
    first = tiles(1, first, keyval_term[:RANK])
    first = tiles(1, first, keyval_term[RANK:])
    first = tiles(1, first, out_term)
    first = tiles(1, first, up)
    for t in range(first, 96):
        put(1, t, jnp.zeros((RANK, ROWS), BF))
    kept_ref[...] = both[core]
    sent_ref[...] = both[1 - core]


def unpack_kernel(kept_ref, sent_ref, down_ref, query_ref, keyval_ref, out_down_ref, out_up_ref, both):
    core = lax.axis_index("core")
    both[core] = kept_ref[...]
    both[1 - core] = sent_ref[...]

    def get(half, tile):
        return both[half, tile // 3, pl.ds(tile % 3 * RANK, RANK), :]

    for c in range(3):
        for t in range(WIDTH // ROWS):
            down_ref[c, :, pl.ds(t * ROWS, ROWS)] = get(0, c * (WIDTH // ROWS) + t)
    first = 0
    for ref, lead in ((query_ref, None), (keyval_ref, 0), (keyval_ref, 1), (out_down_ref, None), (out_up_ref, None)):
        count = ref.shape[-1] // ROWS
        for t in range(count):
            if lead is None:
                ref[:, pl.ds(t * ROWS, ROWS)] = get(1, first + t)
            else:
                ref[lead, :, pl.ds(t * ROWS, ROWS)] = get(1, first + t)
        first += count


VMEM = pl.BlockSpec(memory_space=pltpu.VMEM)


def call(kernel, name, outs, args, scratch=(), flops=0, size=0, limit=32 << 20, kind=None):
    specs = [kind or VMEM] * len(args)
    return pl.pallas_call(
        kernel,
        name=name,
        out_shape=outs,
        in_specs=specs,
        out_specs=jax.tree.map(lambda _: VMEM, outs),
        scratch_shapes=list(scratch),
        compiler_params=pltpu.CompilerParams(vmem_limit_bytes=limit),
        cost_estimate=pl.CostEstimate(flops=flops, bytes_accessed=size, transcendentals=0),
    )(*args)


def shape(dims, dtype=BF):
    return jax.ShapeDtypeStruct(dims, dtype)


def chain_pairs(length):
    up = [[(i, i + 1) for i in range(step, length - 1)] for step in range(SPAN // 2)]
    down, wanted = [], {(place - 5, place) for place in range(5, length)}
    for _ in range(2):
        down.insert(0, sorted(((place + 1) % length, place) for _, place in wanted))
        earlier = {(block, (place + 1) % length) for block, place in wanted}
        offset = 5 + len(down)
        wanted = earlier | {(place - offset, place) for place in range(offset, length)}
    down.insert(0, sorted(wanted))
    return up, down


def per_device(
    normed_input,
    document_index,
    frozen_query_state,
    frozen_keyvalue_weight,
    layer_output_gradient,
    frozen_output_gradient,
    adapter_down_weight,
    query_up_weight,
    keyvalue_up_weight,
    output_down_weight,
    output_up_weight,
):
    x = normed_input[0]
    outgrad = layer_output_gradient[0]
    down = adapter_down_weight.transpose(0, 2, 1).reshape(3 * RANK, WIDTH)
    out_down = output_down_weight.T
    seq = ("x", "y")
    length = lax.axis_size("x") * lax.axis_size("y")

    low, pack = call(
        keyval_kernel, "keyval", (shape((3 * RANK, ROWS)), shape((PACK_ROWS, 2 * KEY_COLUMNS))),
        (x, down, frozen_keyvalue_weight[0], keyvalue_up_weight, document_index),
        scratch=(
            pltpu.VMEM((ROWS, WIDTH), BF),
            pltpu.VMEM((3 * RANK, WIDTH), BF),
            pltpu.VMEM((ROWS, 2 * KEY_COLUMNS), BF),
            pltpu.VMEM((2, RANK, KEY_COLUMNS), BF),
            pltpu.VMEM((1, ROWS), jnp.int32),
            pltpu.SemaphoreType.DMA((5,)),
        ),
        flops=10**8, size=2 * 10**6, limit=56 << 20, kind=pl.BlockSpec(memory_space=pl.ANY),
    )

    blocks = {0: pack}
    up, down = chain_pairs(length)
    for step in range(1, 5):
        blocks[step] = lax.ppermute(blocks[step - 1], seq, up[step - 1])
        if step < 4:
            blocks[8 - step] = lax.ppermute(blocks[(9 - step) % SPAN], seq, down[step - 1])

    q, grad, back_out = call(
        query_kernel, "query",
        (shape((ROWS, QUERY_COLUMNS)), shape((ROWS, QUERY_COLUMNS)), shape((RANK, ROWS))),
        (low, frozen_query_state[0], query_up_weight, outgrad, output_up_weight, frozen_output_gradient[0], out_down),
        flops=10**8, size=4 * 10**6,
    )

    window = SPAN * ROWS
    parts, back_query, low_out, query_term, keyval_term, out_term = call(
        attention_kernel, "attention",
        (
            shape((DEVICES, 2 * RANK, ROWS)),
            shape((RANK, ROWS)),
            shape((RANK, ROWS)),
            shape((RANK, QUERY_COLUMNS), F32),
            shape((2 * RANK, KEY_COLUMNS), F32),
            shape((RANK, QUERY_COLUMNS), F32),
        ),
        (low, q, grad, back_out, query_up_weight, keyvalue_up_weight, out_down,
         *[blocks[o] for o in range(SPAN)]),
        scratch=(
            pltpu.VMEM((window, GROUP * ROWS), F32),
            pltpu.VMEM((window, HEAD_SIZE), BF),
            pltpu.VMEM((window, HEAD_SIZE), BF),
            pltpu.VMEM((RANK, window), BF),
            pltpu.VMEM((RANK, window), BF),
            pltpu.VMEM((2 * RANK, window), F32),
        ),
        flops=4 * 10**9, size=4 * 10**6,
    )

    parts = lax.all_to_all(parts, seq, 0, 0, tiled=False)

    half = (length, 3 * RANK, ROWS)
    kept, sent = call(
        term_kernel, "terms", (shape(half), shape(half)),
        (x, outgrad, back_query, parts, low_out, query_term, keyval_term, out_term),
        scratch=(pltpu.VMEM((2, *half), BF),),
        flops=10**8, size=4 * 10**6,
    )

    swap = [(0, 1), (1, 0)]
    total = (kept.astype(F32) + lax.ppermute(sent, "core", swap).astype(F32)).astype(BF)
    total = lax.all_to_all(total, seq, 0, 0, tiled=False)
    total = jnp.sum(total.astype(F32), axis=0).astype(BF)
    depth = lax.axis_size("z")
    total = lax.all_to_all(jnp.broadcast_to(total, (depth, *total.shape)), "z", 0, 0, tiled=False)
    scale = 0.5 / (depth * lax.axis_size("core"))
    total = (jnp.sum(total.astype(F32), axis=0) * scale).astype(BF)
    total = lax.all_to_all(jnp.broadcast_to(total, half), seq, 0, 0, tiled=False)
    other = lax.ppermute(total, "core", swap)

    lora, query_up, keyval_up, output_down, output_up = call(
        unpack_kernel, "unpack",
        (
            shape((3, RANK, WIDTH)),
            shape((RANK, QUERY_COLUMNS)),
            shape((2, RANK, KEY_COLUMNS)),
            shape((RANK, QUERY_COLUMNS)),
            shape((RANK, WIDTH)),
        ),
        (total, other),
        scratch=(pltpu.VMEM((2, *half), BF),),
        size=2 * 10**6,
    )
    return lora.transpose(0, 2, 1), query_up, keyval_up, output_down.T, output_up


def solution(mesh):
    named = Mesh(mesh.devices.reshape(8, 2, 4, 8), ("z", "core", "x", "y"))
    rep, seq = ("z", "core"), ("x", "y")
    split = P(rep, seq, None)
    placed = (split, P(rep, seq), split, split, split, split, P(), P(), P(), P(), P())
    return jax.shard_map(
        per_device, mesh=named, in_specs=placed, out_specs=(P(), P(), P(), P(), P()), check_vma=False
    )
```

```python
import jax
import jax.numpy as jnp
from jax import lax
from jax.experimental import pallas as pl
from jax.experimental.pallas import tpu as pltpu
from jax.sharding import Mesh, PartitionSpec as P

QUERY_HEADS = 16
KEY_HEADS = 4
HEAD_SIZE = 128
KEY_COLUMNS = 512
ROWS = 128
RANK = 16
SPAN = 8
GROUP = QUERY_HEADS // KEY_HEADS
WIDTH = 4096
QUERY_COLUMNS = QUERY_HEADS * HEAD_SIZE
PACK_ROWS = ROWS + 16
BF = jnp.bfloat16
F32 = jnp.float32
INVERSE = 1.0 / HEAD_SIZE**0.5
DEVICES = 32
LOG2E = 1.4426950408889634

NT = (((1,), (1,)), ((), ()))
TN = (((0,), (0,)), ((), ()))
NN = (((1,), (0,)), ((), ()))


def dot(a, b, dims=NN):
    return lax.dot_general(a, b, dims, preferred_element_type=F32)


def keyval_kernel(x_any, down_any, keyval_any, up_any, doc_any, low_ref, pack_ref,
                  x_ref, down_ref, keyval_ref, up_ref, doc_ref, sems):
    pairs = ((x_any, x_ref), (down_any, down_ref), (keyval_any, keyval_ref), (up_any, up_ref), (doc_any, doc_ref))
    copies = [pltpu.make_async_copy(a, b, sems.at[i]) for i, (a, b) in enumerate(pairs)]
    for copy in copies:
        copy.start()
    copies[0].wait()
    copies[1].wait()
    low = dot(down_ref[...], x_ref[...], NT).astype(BF)
    low_ref[...] = low
    for copy in copies[2:]:
        copy.wait()
    for c in range(2):
        part = pl.ds(c * KEY_COLUMNS, KEY_COLUMNS)
        delta = dot(low[(c + 1) * RANK : (c + 2) * RANK], up_ref[c], TN)
        pack_ref[pl.ds(0, ROWS), part] = (
            keyval_ref[:, part].astype(F32) + 0.5 * delta
        ).astype(BF)
    documents = jnp.broadcast_to(doc_ref[...].astype(F32), (RANK, ROWS)).astype(BF)
    pack_ref[pl.ds(ROWS, RANK), :] = jnp.concatenate(
        [low[RANK : 2 * RANK], low[2 * RANK :], documents, jnp.zeros((RANK, 5 * ROWS), BF)], axis=1
    )


def query_kernel(low_ref, query_ref, query_up_ref, outgrad_ref, out_up_ref, frozen_ref, out_down_ref,
                 q_ref, grad_ref, back_out_ref):
    q_ref[...] = (
        query_ref[...].astype(F32) + 0.5 * dot(low_ref[pl.ds(0, RANK), :], query_up_ref[...], TN)
    ).astype(BF)
    back_out = dot(out_up_ref[...], outgrad_ref[...], NT).astype(BF)
    back_out_ref[...] = back_out
    grad_ref[...] = (
        frozen_ref[...].astype(F32) + 0.5 * dot(back_out, out_down_ref[...], TN)
    ).astype(BF)


def attention_kernel(low_ref, q_ref, grad_ref, back_out_ref, query_up_ref, up_ref,
                     out_down_ref, *rest):
    blocks = rest[:SPAN]
    parts_ref, back_query_ref, low_out_ref, query_term_ref, keyval_term_ref, out_term_ref = rest[SPAN : SPAN + 6]
    bias, keys, values, low_keys, low_values, back_parts = rest[SPAN + 6 :]
    position = lax.axis_index("x") * SPAN + lax.axis_index("y")
    core = lax.axis_index("core")
    offsets = [0] + [s + core * (SPAN - 2 * s) for s in (1, 2, 3, 4)] + [SPAN - s + core * (2 * s - SPAN) for s in (1, 2, 3)]
    own = blocks[0][pl.ds(ROWS, RANK), pl.ds(2 * ROWS, ROWS)][:1]
    own = jnp.broadcast_to(own.astype(F32), (ROWS, ROWS))
    row = lax.broadcasted_iota(jnp.int32, (ROWS, ROWS), 0)
    col = lax.broadcasted_iota(jnp.int32, (ROWS, ROWS), 1)
    for o in range(SPAN):
        span = pl.ds(o * ROWS, ROWS)
        extra = blocks[o][pl.ds(ROWS, RANK), :]
        low_keys[:, span] = extra[:, :ROWS]
        low_values[:, span] = extra[:, ROWS : 2 * ROWS]
        document = jnp.transpose(jnp.broadcast_to(extra[:1, 2 * ROWS : 3 * ROWS].astype(F32), (ROWS, ROWS)))
        seen = own == document
        if o == 0:
            seen = seen & (row <= col)
        else:
            seen = seen & (jnp.broadcast_to(position - offsets[o], (ROWS, ROWS)) >= 0)
        one = jnp.where(seen, 0.0, -1e30)
        for i in range(GROUP):
            bias[span, pl.ds(i*ROWS, ROWS)] = one
    back_parts[...] = jnp.zeros_like(back_parts)
    low_zero = low_ref[pl.ds(0, RANK), :]
    back_out = back_out_ref[...]

    def one_group(g, sums):
        back_query, low_out = sums
        at = pl.ds(pl.multiple_of(g * HEAD_SIZE, HEAD_SIZE), HEAD_SIZE)
        value_at = pl.ds(pl.multiple_of(KEY_COLUMNS + g * HEAD_SIZE, HEAD_SIZE), HEAD_SIZE)
        for o in range(SPAN):
            span = pl.ds(o * ROWS, ROWS)
            keys[span, :] = blocks[o][pl.ds(0, ROWS), at]
            values[span, :] = blocks[o][pl.ds(0, ROWS), value_at]
        heads = [pl.ds(pl.multiple_of((g * GROUP + i) * HEAD_SIZE, HEAD_SIZE), HEAD_SIZE) for i in range(GROUP)]
        q = jnp.concatenate([q_ref[:, h] for h in heads], axis=0)
        grad = jnp.concatenate([grad_ref[:, h] for h in heads], axis=0)
        qT = jnp.transpose(q.astype(F32))
        gradT = jnp.transpose(grad.astype(F32))
        k, v = keys[...], values[...]
        scores = dot(k, qT.astype(BF)) * (INVERSE * LOG2E) + bias[...]
        powers = jnp.exp2(scores - jnp.max(scores, axis=0, keepdims=True))
        recip = 1.0 / jnp.sum(powers, axis=0, keepdims=True)
        powers = powers.astype(BF)
        attn = (dot(v, powers, TN) * recip).astype(BF)
        delta = jnp.sum(gradT * attn.astype(F32), axis=0, keepdims=True)
        dprobs = dot(v, gradT.astype(BF))
        dscores = powers * (dprobs - delta).astype(BF)
        dq = (dot(k, dscores, TN) * (recip * INVERSE)).astype(BF)
        scaled_q = jnp.transpose(qT * (recip * INVERSE)).astype(BF)
        scaled_grad = jnp.transpose(gradT * recip).astype(BF)
        dkeys = dot(dscores, scaled_q).astype(BF)
        dvalues = dot(powers, scaled_grad).astype(BF)
        back_parts[pl.ds(0, RANK), :] += dot(up_ref[0, :, at], dkeys, NT)
        back_parts[pl.ds(RANK, RANK), :] += dot(up_ref[1, :, at], dvalues, NT)
        keyval_term_ref[pl.ds(0, RANK), at] = dot(low_keys[...], dkeys)
        keyval_term_ref[pl.ds(RANK, RANK), at] = dot(low_values[...], dvalues)
        for i, h in enumerate(heads):
            mine = slice(i * ROWS, (i + 1) * ROWS)
            query_term_ref[:, h] = dot(low_zero, dq[:, mine], NT)
            out_term_ref[:, h] = dot(back_out, attn[:, mine], NT)
            back_query = back_query + dot(query_up_ref[:, h], dq[:, mine])
            low_out = low_out + dot(out_down_ref[:, h], attn[:, mine])
        return back_query, low_out

    zero = jnp.zeros((RANK, ROWS), F32)
    back_query, low_out = lax.fori_loop(0, KEY_HEADS, one_group, (zero, zero), unroll=True)
    back_query_ref[...] = back_query.astype(BF)
    low_out_ref[...] = low_out.astype(BF)
    parts_ref[...] = jnp.zeros_like(parts_ref)
    for o in range(SPAN):
        parts_ref[lax.rem(position + (DEVICES - offsets[o]), DEVICES)] = back_parts[:, pl.ds(o * ROWS, ROWS)].astype(BF)


def term_kernel(x_ref, outgrad_ref, back_query_ref, parts_ref, low_out_ref,
                query_term_ref, keyval_term_ref, out_term_ref, kept_ref, sent_ref, both):
    core = lax.axis_index("core")
    back_keyval = parts_ref[0].astype(F32)
    for i in range(1, DEVICES):
        back_keyval = back_keyval + parts_ref[i].astype(F32)
    back = jnp.concatenate([back_query_ref[...], back_keyval.astype(BF)], axis=0)
    down = dot(back, x_ref[...]).astype(BF)
    up = dot(low_out_ref[...], outgrad_ref[...]).astype(BF)
    query_term = query_term_ref[...].astype(BF)
    keyval_term = keyval_term_ref[...].astype(BF)
    out_term = out_term_ref[...].astype(BF)

    def put(half, tile, value):
        both[half, tile // 3, pl.ds(tile % 3 * RANK, RANK), :] = value

    def tiles(half, first, array):
        for t in range(array.shape[1] // ROWS):
            put(half, first + t, array[:, t * ROWS : (t + 1) * ROWS])
        return first + array.shape[1] // ROWS

    first = 0
    for c in range(3):
        first = tiles(0, first, down[c * RANK : (c + 1) * RANK])
    first = tiles(1, 0, query_term)
    first = tiles(1, first, keyval_term[:RANK])
    first = tiles(1, first, keyval_term[RANK:])
    first = tiles(1, first, out_term)
    first = tiles(1, first, up)
    for t in range(first, 96):
        put(1, t, jnp.zeros((RANK, ROWS), BF))
    kept_ref[...] = both[core]
    sent_ref[...] = both[1 - core]


def unpack_kernel(kept_ref, sent_ref, down_ref, query_ref, keyval_ref, out_down_ref, out_up_ref, both):
    core = lax.axis_index("core")
    both[core] = kept_ref[...]
    both[1 - core] = sent_ref[...]

    def get(half, tile):
        return both[half, tile // 3, pl.ds(tile % 3 * RANK, RANK), :]

    for c in range(3):
        for t in range(WIDTH // ROWS):
            down_ref[c, :, pl.ds(t * ROWS, ROWS)] = get(0, c * (WIDTH // ROWS) + t)
    first = 0
    for ref, lead in ((query_ref, None), (keyval_ref, 0), (keyval_ref, 1), (out_down_ref, None), (out_up_ref, None)):
        count = ref.shape[-1] // ROWS
        for t in range(count):
            if lead is None:
                ref[:, pl.ds(t * ROWS, ROWS)] = get(1, first + t)
            else:
                ref[lead, :, pl.ds(t * ROWS, ROWS)] = get(1, first + t)
        first += count


VMEM = pl.BlockSpec(memory_space=pltpu.VMEM)


def call(kernel, name, outs, args, scratch=(), flops=0, size=0, limit=32 << 20, kind=None):
    specs = [kind or VMEM] * len(args)
    return pl.pallas_call(
        kernel,
        name=name,
        out_shape=outs,
        in_specs=specs,
        out_specs=jax.tree.map(lambda _: VMEM, outs),
        scratch_shapes=list(scratch),
        compiler_params=pltpu.CompilerParams(vmem_limit_bytes=limit),
        cost_estimate=pl.CostEstimate(flops=flops, bytes_accessed=size, transcendentals=0),
    )(*args)


def shape(dims, dtype=BF):
    return jax.ShapeDtypeStruct(dims, dtype)


def pairs_up(length, steps):
    return [[(i, i + 1) for i in range(step, length - 1)] for step in range(steps)]


def pairs_down(length, steps):
    last = SPAN - steps
    pairs, wanted = [], {(place - last, place) for place in range(last, length)}
    for offset in range(last + 1, SPAN):
        pairs.insert(0, sorted(((place + 1) % length, place) for _, place in wanted))
        wanted = {(block, (place + 1) % length) for block, place in wanted}
        wanted |= {(place - offset, place) for place in range(offset, length)}
    return [sorted(wanted)] + pairs


def both_cores(length, first, second):
    return [a + [(i + length, j + length) for i, j in b] for a, b in zip(first, second, strict=True)]


def per_device(
    normed_input,
    document_index,
    frozen_query_state,
    frozen_keyvalue_weight,
    layer_output_gradient,
    frozen_output_gradient,
    adapter_down_weight,
    query_up_weight,
    keyvalue_up_weight,
    output_down_weight,
    output_up_weight,
):
    x = normed_input[0]
    outgrad = layer_output_gradient[0]
    down = adapter_down_weight.transpose(0, 2, 1).reshape(3 * RANK, WIDTH)
    out_down = output_down_weight.T
    seq = ("x", "y")
    length = lax.axis_size("x") * lax.axis_size("y")

    low, pack = call(
        keyval_kernel, "keyval", (shape((3 * RANK, ROWS)), shape((PACK_ROWS, 2 * KEY_COLUMNS))),
        (x, down, frozen_keyvalue_weight[0], keyvalue_up_weight, document_index),
        scratch=(
            pltpu.VMEM((ROWS, WIDTH), BF),
            pltpu.VMEM((3 * RANK, WIDTH), BF),
            pltpu.VMEM((ROWS, 2 * KEY_COLUMNS), BF),
            pltpu.VMEM((2, RANK, KEY_COLUMNS), BF),
            pltpu.VMEM((1, ROWS), jnp.int32),
            pltpu.SemaphoreType.DMA((5,)),
        ),
        flops=10**8, size=2 * 10**6, limit=56 << 20, kind=pl.BlockSpec(memory_space=pl.ANY),
    )

    half_span = SPAN // 2
    long = both_cores(length, pairs_up(length, half_span), pairs_down(length, half_span))
    short = both_cores(length, pairs_down(length, half_span - 1), pairs_up(length, half_span - 1))
    places = ("core", *seq)
    first, second = [pack], [pack]
    for step in range(half_span):
        first.append(lax.ppermute(first[-1], places, long[step]))
        if step < half_span - 1:
            second.append(lax.ppermute(second[-1], places, short[step]))
    blocks = first + second[1:]

    q, grad, back_out = call(
        query_kernel, "query",
        (shape((ROWS, QUERY_COLUMNS)), shape((ROWS, QUERY_COLUMNS)), shape((RANK, ROWS))),
        (low, frozen_query_state[0], query_up_weight, outgrad, output_up_weight, frozen_output_gradient[0], out_down),
        flops=10**8, size=4 * 10**6,
    )

    window = SPAN * ROWS
    parts, back_query, low_out, query_term, keyval_term, out_term = call(
        attention_kernel, "attention",
        (
            shape((DEVICES, 2 * RANK, ROWS)),
            shape((RANK, ROWS)),
            shape((RANK, ROWS)),
            shape((RANK, QUERY_COLUMNS), F32),
            shape((2 * RANK, KEY_COLUMNS), F32),
            shape((RANK, QUERY_COLUMNS), F32),
        ),
        (low, q, grad, back_out, query_up_weight, keyvalue_up_weight, out_down,
         *blocks),
        scratch=(
            pltpu.VMEM((window, GROUP * ROWS), F32),
            pltpu.VMEM((window, HEAD_SIZE), BF),
            pltpu.VMEM((window, HEAD_SIZE), BF),
            pltpu.VMEM((RANK, window), BF),
            pltpu.VMEM((RANK, window), BF),
            pltpu.VMEM((2 * RANK, window), F32),
        ),
        flops=4 * 10**9, size=4 * 10**6,
    )

    parts = lax.all_to_all(parts, seq, 0, 0, tiled=False)

    half = (length, 3 * RANK, ROWS)
    kept, sent = call(
        term_kernel, "terms", (shape(half), shape(half)),
        (x, outgrad, back_query, parts, low_out, query_term, keyval_term, out_term),
        scratch=(pltpu.VMEM((2, *half), BF),),
        flops=10**8, size=4 * 10**6,
    )

    swap = [(0, 1), (1, 0)]
    total = (kept.astype(F32) + lax.ppermute(sent, "core", swap).astype(F32)).astype(BF)
    total = lax.all_to_all(total, seq, 0, 0, tiled=False)
    total = jnp.sum(total.astype(F32), axis=0).astype(BF)
    depth = lax.axis_size("z")
    total = lax.all_to_all(jnp.broadcast_to(total, (depth, *total.shape)), "z", 0, 0, tiled=False)
    scale = 0.5 / (depth * lax.axis_size("core"))
    total = (jnp.sum(total.astype(F32), axis=0) * scale).astype(BF)
    total = lax.all_to_all(jnp.broadcast_to(total, half), seq, 0, 0, tiled=False)
    other = lax.ppermute(total, "core", swap)

    lora, query_up, keyval_up, output_down, output_up = call(
        unpack_kernel, "unpack",
        (
            shape((3, RANK, WIDTH)),
            shape((RANK, QUERY_COLUMNS)),
            shape((2, RANK, KEY_COLUMNS)),
            shape((RANK, QUERY_COLUMNS)),
            shape((RANK, WIDTH)),
        ),
        (total, other),
        scratch=(pltpu.VMEM((2, *half), BF),),
        size=2 * 10**6,
    )
    return lora.transpose(0, 2, 1), query_up, keyval_up, output_down.T, output_up


def solution(mesh):
    named = Mesh(mesh.devices.reshape(8, 2, 4, 8), ("z", "core", "x", "y"))
    rep, seq = ("z", "core"), ("x", "y")
    split = P(rep, seq, None)
    placed = (split, P(rep, seq), split, split, split, split, P(), P(), P(), P(), P())
    return jax.shard_map(
        per_device, mesh=named, in_specs=placed, out_specs=(P(), P(), P(), P(), P()), check_vma=False
    )
```

```python
import functools

import jax
import jax.numpy as jnp
from jax import lax
from jax.experimental import pallas as pl
from jax.experimental.pallas import tpu as pltpu
from jax.sharding import Mesh, PartitionSpec as P

QUERY_HEADS = 16
KEY_HEADS = 4
HEAD_SIZE = 128
KEY_COLUMNS = 512
ROWS = 128
RANK = 16
SPAN = 8
GROUP = QUERY_HEADS // KEY_HEADS
WIDTH = 4096
QUERY_COLUMNS = QUERY_HEADS * HEAD_SIZE
PACK_ROWS = ROWS + 16
BF = jnp.bfloat16
F32 = jnp.float32
INVERSE = 1.0 / HEAD_SIZE**0.5
DEVICES = 32
LOG2E = 1.4426950408889634

NT = (((1,), (1,)), ((), ()))
TN = (((0,), (0,)), ((), ()))
NN = (((1,), (0,)), ((), ()))


def dot(a, b, dims=NN):
    return lax.dot_general(a, b, dims, preferred_element_type=F32)


def keyval_kernel(x_any, down_any, keyval_any, up_any, doc_any, low_ref, pack_ref,
                  x_ref, down_ref, keyval_ref, up_ref, doc_ref, sems):
    pairs = ((x_any, x_ref), (down_any, down_ref), (keyval_any, keyval_ref), (up_any, up_ref), (doc_any, doc_ref))
    copies = [pltpu.make_async_copy(a, b, sems.at[i]) for i, (a, b) in enumerate(pairs)]
    for copy in copies:
        copy.start()
    copies[0].wait()
    copies[1].wait()
    low = dot(down_ref[...], x_ref[...], NT).astype(BF)
    low_ref[...] = low
    for copy in copies[2:]:
        copy.wait()
    for c in range(2):
        part = pl.ds(c * KEY_COLUMNS, KEY_COLUMNS)
        delta = dot(low[(c + 1) * RANK : (c + 2) * RANK], up_ref[c], TN)
        pack_ref[pl.ds(0, ROWS), part] = (
            keyval_ref[:, part].astype(F32) + 0.5 * delta
        ).astype(BF)
    documents = jnp.broadcast_to(doc_ref[...].astype(F32), (RANK, ROWS)).astype(BF)
    pack_ref[pl.ds(ROWS, RANK), :] = jnp.concatenate(
        [low[RANK : 2 * RANK], low[2 * RANK :], documents, jnp.zeros((RANK, 5 * ROWS), BF)], axis=1
    )


def query_kernel(low_ref, query_ref, query_up_ref, outgrad_ref, out_up_ref, frozen_ref, out_down_ref,
                 q_ref, grad_ref, back_out_ref):
    q_ref[...] = (
        query_ref[...].astype(F32) + 0.5 * dot(low_ref[pl.ds(0, RANK), :], query_up_ref[...], TN)
    ).astype(BF)
    back_out = dot(out_up_ref[...], outgrad_ref[...], NT).astype(BF)
    back_out_ref[...] = back_out
    grad_ref[...] = (
        frozen_ref[...].astype(F32) + 0.5 * dot(back_out, out_down_ref[...], TN)
    ).astype(BF)


def attention_kernel(low_ref, q_ref, grad_ref, back_out_ref, query_up_ref, up_ref,
                     out_down_ref, *rest):
    blocks = rest[:SPAN]
    parts_ref, back_query_ref, low_out_ref, query_term_ref, keyval_term_ref, out_term_ref = rest[SPAN : SPAN + 6]
    bias, keys, values, low_keys, low_values, back_parts = rest[SPAN + 6 :]
    position = lax.axis_index("x") * SPAN + lax.axis_index("y")
    own = blocks[0][pl.ds(ROWS, RANK), pl.ds(2 * ROWS, ROWS)][:1]
    own = jnp.broadcast_to(own.astype(F32), (ROWS, ROWS))
    row = lax.broadcasted_iota(jnp.int32, (ROWS, ROWS), 0)
    col = lax.broadcasted_iota(jnp.int32, (ROWS, ROWS), 1)
    for o in range(SPAN):
        span = pl.ds(o * ROWS, ROWS)
        extra = blocks[o][pl.ds(ROWS, RANK), :]
        low_keys[:, span] = extra[:, :ROWS]
        low_values[:, span] = extra[:, ROWS : 2 * ROWS]
        document = jnp.transpose(jnp.broadcast_to(extra[:1, 2 * ROWS : 3 * ROWS].astype(F32), (ROWS, ROWS)))
        seen = own == document
        if o == 0:
            seen = seen & (row <= col)
        else:
            seen = seen & (jnp.broadcast_to(position, (ROWS, ROWS)) >= o)
        one = jnp.where(seen, 0.0, -1e30)
        for i in range(GROUP):
            bias[span, pl.ds(i*ROWS, ROWS)] = one
    back_parts[...] = jnp.zeros_like(back_parts)
    low_zero = low_ref[pl.ds(0, RANK), :]
    back_out = back_out_ref[...]

    def one_group(count, g, sums):
        back_query, low_out = sums
        near = pl.ds(0, count * ROWS)
        at = pl.ds(pl.multiple_of(g * HEAD_SIZE, HEAD_SIZE), HEAD_SIZE)
        value_at = pl.ds(pl.multiple_of(KEY_COLUMNS + g * HEAD_SIZE, HEAD_SIZE), HEAD_SIZE)
        for o in range(count):
            span = pl.ds(o * ROWS, ROWS)
            keys[span, :] = blocks[o][pl.ds(0, ROWS), at]
            values[span, :] = blocks[o][pl.ds(0, ROWS), value_at]
        heads = [pl.ds(pl.multiple_of((g * GROUP + i) * HEAD_SIZE, HEAD_SIZE), HEAD_SIZE) for i in range(GROUP)]
        q = jnp.concatenate([q_ref[:, h] for h in heads], axis=0)
        grad = jnp.concatenate([grad_ref[:, h] for h in heads], axis=0)
        qT = jnp.transpose(q.astype(F32))
        gradT = jnp.transpose(grad.astype(F32))
        k, v = keys[near, :], values[near, :]
        scores = dot(k, qT.astype(BF)) * (INVERSE * LOG2E) + bias[near, :]
        powers = jnp.exp2(scores - jnp.max(scores, axis=0, keepdims=True))
        recip = 1.0 / jnp.sum(powers, axis=0, keepdims=True)
        powers = powers.astype(BF)
        attn = (dot(v, powers, TN) * recip).astype(BF)
        delta = jnp.sum(gradT * attn.astype(F32), axis=0, keepdims=True)
        dprobs = dot(v, gradT.astype(BF))
        dscores = powers * (dprobs - delta).astype(BF)
        dq = (dot(k, dscores, TN) * (recip * INVERSE)).astype(BF)
        scaled_q = jnp.transpose(qT * (recip * INVERSE)).astype(BF)
        scaled_grad = jnp.transpose(gradT * recip).astype(BF)
        dkeys = dot(dscores, scaled_q).astype(BF)
        dvalues = dot(powers, scaled_grad).astype(BF)
        back_parts[pl.ds(0, RANK), near] += dot(up_ref[0, :, at], dkeys, NT)
        back_parts[pl.ds(RANK, RANK), near] += dot(up_ref[1, :, at], dvalues, NT)
        keyval_term_ref[pl.ds(0, RANK), at] = dot(low_keys[:, near], dkeys)
        keyval_term_ref[pl.ds(RANK, RANK), at] = dot(low_values[:, near], dvalues)
        for i, h in enumerate(heads):
            mine = slice(i * ROWS, (i + 1) * ROWS)
            query_term_ref[:, h] = dot(low_zero, dq[:, mine], NT)
            out_term_ref[:, h] = dot(back_out, attn[:, mine], NT)
            back_query = back_query + dot(query_up_ref[:, h], dq[:, mine])
            low_out = low_out + dot(out_down_ref[:, h], attn[:, mine])
        return back_query, low_out

    def all_groups(count):
        zero = jnp.zeros((RANK, ROWS), F32)
        back_query, low_out = lax.fori_loop(
            0, KEY_HEADS, functools.partial(one_group, count), (zero, zero), unroll=True
        )
        back_query_ref[...] = back_query.astype(BF)
        low_out_ref[...] = low_out.astype(BF)

    beyond_two = jnp.max(bias[pl.ds(2 * ROWS, 6 * ROWS), pl.ds(0, ROWS)]) > -1.0
    beyond_four = jnp.max(bias[pl.ds(4 * ROWS, 4 * ROWS), pl.ds(0, ROWS)]) > -1.0
    pl.when(jnp.logical_not(beyond_two))(lambda: all_groups(2))
    pl.when(jnp.logical_and(beyond_two, jnp.logical_not(beyond_four)))(lambda: all_groups(4))
    pl.when(beyond_four)(lambda: all_groups(8))
    parts_ref[...] = jnp.zeros_like(parts_ref)
    for o in range(SPAN):
        parts_ref[lax.rem(position + (DEVICES - o), DEVICES)] = back_parts[:, pl.ds(o * ROWS, ROWS)].astype(BF)


def term_kernel(x_ref, outgrad_ref, back_query_ref, parts_ref, low_out_ref,
                query_term_ref, keyval_term_ref, out_term_ref, kept_ref, sent_ref, both):
    core = lax.axis_index("core")
    back_keyval = parts_ref[0].astype(F32)
    for i in range(1, DEVICES):
        back_keyval = back_keyval + parts_ref[i].astype(F32)
    back = jnp.concatenate([back_query_ref[...], back_keyval.astype(BF)], axis=0)
    down = dot(back, x_ref[...]).astype(BF)
    up = dot(low_out_ref[...], outgrad_ref[...]).astype(BF)
    query_term = query_term_ref[...].astype(BF)
    keyval_term = keyval_term_ref[...].astype(BF)
    out_term = out_term_ref[...].astype(BF)

    def put(half, tile, value):
        both[half, tile // 3, pl.ds(tile % 3 * RANK, RANK), :] = value

    def tiles(half, first, array):
        for t in range(array.shape[1] // ROWS):
            put(half, first + t, array[:, t * ROWS : (t + 1) * ROWS])
        return first + array.shape[1] // ROWS

    first = 0
    for c in range(3):
        first = tiles(0, first, down[c * RANK : (c + 1) * RANK])
    first = tiles(1, 0, query_term)
    first = tiles(1, first, keyval_term[:RANK])
    first = tiles(1, first, keyval_term[RANK:])
    first = tiles(1, first, out_term)
    first = tiles(1, first, up)
    for t in range(first, 96):
        put(1, t, jnp.zeros((RANK, ROWS), BF))
    kept_ref[...] = both[core]
    sent_ref[...] = both[1 - core]


def unpack_kernel(kept_ref, sent_ref, down_ref, query_ref, keyval_ref, out_down_ref, out_up_ref, both):
    core = lax.axis_index("core")
    both[core] = kept_ref[...]
    both[1 - core] = sent_ref[...]

    def get(half, tile):
        return both[half, tile // 3, pl.ds(tile % 3 * RANK, RANK), :]

    for c in range(3):
        for t in range(WIDTH // ROWS):
            down_ref[c, :, pl.ds(t * ROWS, ROWS)] = get(0, c * (WIDTH // ROWS) + t)
    first = 0
    for ref, lead in ((query_ref, None), (keyval_ref, 0), (keyval_ref, 1), (out_down_ref, None), (out_up_ref, None)):
        count = ref.shape[-1] // ROWS
        for t in range(count):
            if lead is None:
                ref[:, pl.ds(t * ROWS, ROWS)] = get(1, first + t)
            else:
                ref[lead, :, pl.ds(t * ROWS, ROWS)] = get(1, first + t)
        first += count


VMEM = pl.BlockSpec(memory_space=pltpu.VMEM)


def call(kernel, name, outs, args, scratch=(), flops=0, size=0, limit=32 << 20, kind=None):
    specs = [kind or VMEM] * len(args)
    return pl.pallas_call(
        kernel,
        name=name,
        out_shape=outs,
        in_specs=specs,
        out_specs=jax.tree.map(lambda _: VMEM, outs),
        scratch_shapes=list(scratch),
        compiler_params=pltpu.CompilerParams(vmem_limit_bytes=limit),
        cost_estimate=pl.CostEstimate(flops=flops, bytes_accessed=size, transcendentals=0),
    )(*args)


def shape(dims, dtype=BF):
    return jax.ShapeDtypeStruct(dims, dtype)


def chain_pairs(length):
    up = [[(i, i + 1) for i in range(step, length - 1)] for step in range(SPAN // 2)]
    down, wanted = [], {(place - 5, place) for place in range(5, length)}
    for _ in range(2):
        down.insert(0, sorted(((place + 1) % length, place) for _, place in wanted))
        earlier = {(block, (place + 1) % length) for block, place in wanted}
        offset = 5 + len(down)
        wanted = earlier | {(place - offset, place) for place in range(offset, length)}
    down.insert(0, sorted(wanted))
    return up, down


def per_device(
    normed_input,
    document_index,
    frozen_query_state,
    frozen_keyvalue_weight,
    layer_output_gradient,
    frozen_output_gradient,
    adapter_down_weight,
    query_up_weight,
    keyvalue_up_weight,
    output_down_weight,
    output_up_weight,
):
    x = normed_input[0]
    outgrad = layer_output_gradient[0]
    down = adapter_down_weight.transpose(0, 2, 1).reshape(3 * RANK, WIDTH)
    out_down = output_down_weight.T
    seq = ("x", "y")
    length = lax.axis_size("x") * lax.axis_size("y")

    low, pack = call(
        keyval_kernel, "keyval", (shape((3 * RANK, ROWS)), shape((PACK_ROWS, 2 * KEY_COLUMNS))),
        (x, down, frozen_keyvalue_weight[0], keyvalue_up_weight, document_index),
        scratch=(
            pltpu.VMEM((ROWS, WIDTH), BF),
            pltpu.VMEM((3 * RANK, WIDTH), BF),
            pltpu.VMEM((ROWS, 2 * KEY_COLUMNS), BF),
            pltpu.VMEM((2, RANK, KEY_COLUMNS), BF),
            pltpu.VMEM((1, ROWS), jnp.int32),
            pltpu.SemaphoreType.DMA((5,)),
        ),
        flops=10**8, size=2 * 10**6, limit=56 << 20, kind=pl.BlockSpec(memory_space=pl.ANY),
    )

    blocks = {0: pack}
    up, down = chain_pairs(length)
    for step in range(1, 5):
        blocks[step] = lax.ppermute(blocks[step - 1], seq, up[step - 1])
        if step < 4:
            blocks[8 - step] = lax.ppermute(blocks[(9 - step) % SPAN], seq, down[step - 1])

    q, grad, back_out = call(
        query_kernel, "query",
        (shape((ROWS, QUERY_COLUMNS)), shape((ROWS, QUERY_COLUMNS)), shape((RANK, ROWS))),
        (low, frozen_query_state[0], query_up_weight, outgrad, output_up_weight, frozen_output_gradient[0], out_down),
        flops=10**8, size=4 * 10**6,
    )

    window = SPAN * ROWS
    parts, back_query, low_out, query_term, keyval_term, out_term = call(
        attention_kernel, "attention",
        (
            shape((DEVICES, 2 * RANK, ROWS)),
            shape((RANK, ROWS)),
            shape((RANK, ROWS)),
            shape((RANK, QUERY_COLUMNS), F32),
            shape((2 * RANK, KEY_COLUMNS), F32),
            shape((RANK, QUERY_COLUMNS), F32),
        ),
        (low, q, grad, back_out, query_up_weight, keyvalue_up_weight, out_down,
         *[blocks[o] for o in range(SPAN)]),
        scratch=(
            pltpu.VMEM((window, GROUP * ROWS), F32),
            pltpu.VMEM((window, HEAD_SIZE), BF),
            pltpu.VMEM((window, HEAD_SIZE), BF),
            pltpu.VMEM((RANK, window), BF),
            pltpu.VMEM((RANK, window), BF),
            pltpu.VMEM((2 * RANK, window), F32),
        ),
        flops=4 * 10**9, size=4 * 10**6,
    )

    parts = lax.all_to_all(parts, seq, 0, 0, tiled=False)

    half = (length, 3 * RANK, ROWS)
    kept, sent = call(
        term_kernel, "terms", (shape(half), shape(half)),
        (x, outgrad, back_query, parts, low_out, query_term, keyval_term, out_term),
        scratch=(pltpu.VMEM((2, *half), BF),),
        flops=10**8, size=4 * 10**6,
    )

    swap = [(0, 1), (1, 0)]
    total = (kept.astype(F32) + lax.ppermute(sent, "core", swap).astype(F32)).astype(BF)
    total = lax.all_to_all(total, seq, 0, 0, tiled=False)
    total = jnp.sum(total.astype(F32), axis=0).astype(BF)
    depth = lax.axis_size("z")
    total = lax.all_to_all(jnp.broadcast_to(total, (depth, *total.shape)), "z", 0, 0, tiled=False)
    scale = 0.5 / (depth * lax.axis_size("core"))
    total = (jnp.sum(total.astype(F32), axis=0) * scale).astype(BF)
    total = lax.all_to_all(jnp.broadcast_to(total, half), seq, 0, 0, tiled=False)
    other = lax.ppermute(total, "core", swap)

    lora, query_up, keyval_up, output_down, output_up = call(
        unpack_kernel, "unpack",
        (
            shape((3, RANK, WIDTH)),
            shape((RANK, QUERY_COLUMNS)),
            shape((2, RANK, KEY_COLUMNS)),
            shape((RANK, QUERY_COLUMNS)),
            shape((RANK, WIDTH)),
        ),
        (total, other),
        scratch=(pltpu.VMEM((2, *half), BF),),
        size=2 * 10**6,
    )
    return lora.transpose(0, 2, 1), query_up, keyval_up, output_down.T, output_up


def solution(mesh):
    named = Mesh(mesh.devices.reshape(8, 2, 4, 8), ("z", "core", "x", "y"))
    rep, seq = ("z", "core"), ("x", "y")
    split = P(rep, seq, None)
    placed = (split, P(rep, seq), split, split, split, split, P(), P(), P(), P(), P())
    return jax.shard_map(
        per_device, mesh=named, in_specs=placed, out_specs=(P(), P(), P(), P(), P()), check_vma=False
    )
```

```python
import jax
import jax.numpy as jnp
from jax import lax
from jax.experimental import pallas as pl
from jax.experimental.pallas import tpu as pltpu
from jax.sharding import Mesh, PartitionSpec as P

QUERY_HEADS = 16
KEY_HEADS = 4
HEAD_SIZE = 128
KEY_COLUMNS = 512
ROWS = 128
RANK = 16
SPAN = 8
GROUP = QUERY_HEADS // KEY_HEADS
WIDTH = 4096
QUERY_COLUMNS = QUERY_HEADS * HEAD_SIZE
PACK_ROWS = ROWS + 16
BF = jnp.bfloat16
F32 = jnp.float32
INVERSE = 1.0 / HEAD_SIZE**0.5
DEVICES = 32
LOG2E = 1.4426950408889634

NT = (((1,), (1,)), ((), ()))
TN = (((0,), (0,)), ((), ()))
NN = (((1,), (0,)), ((), ()))


def dot(a, b, dims=NN):
    return lax.dot_general(a, b, dims, preferred_element_type=F32)


def keyval_kernel(x_any, down_any, keyval_any, up_any, doc_any, low_ref, pack_ref,
                  x_ref, down_ref, keyval_ref, up_ref, doc_ref, sems):
    pairs = ((x_any, x_ref), (down_any, down_ref), (keyval_any, keyval_ref), (up_any, up_ref), (doc_any, doc_ref))
    copies = [pltpu.make_async_copy(a, b, sems.at[i]) for i, (a, b) in enumerate(pairs)]
    for copy in copies:
        copy.start()
    copies[0].wait()
    copies[1].wait()
    low = dot(down_ref[...], x_ref[...], NT).astype(BF)
    low_ref[...] = low
    for copy in copies[2:]:
        copy.wait()
    for c in range(2):
        part = pl.ds(c * KEY_COLUMNS, KEY_COLUMNS)
        delta = dot(low[(c + 1) * RANK : (c + 2) * RANK], up_ref[c], TN)
        pack_ref[pl.ds(0, ROWS), part] = (
            keyval_ref[:, part].astype(F32) + 0.5 * delta
        ).astype(BF)
    documents = jnp.broadcast_to(doc_ref[...].astype(F32), (RANK, ROWS)).astype(BF)
    pack_ref[pl.ds(ROWS, RANK), :] = jnp.concatenate(
        [low[RANK : 2 * RANK], low[2 * RANK :], documents, jnp.zeros((RANK, 5 * ROWS), BF)], axis=1
    )


def query_kernel(low_ref, query_ref, query_up_ref, outgrad_ref, out_up_ref, frozen_ref, out_down_ref,
                 q_ref, grad_ref, back_out_ref):
    q_ref[...] = (
        query_ref[...].astype(F32) + 0.5 * dot(low_ref[pl.ds(0, RANK), :], query_up_ref[...], TN)
    ).astype(BF)
    back_out = dot(out_up_ref[...], outgrad_ref[...], NT).astype(BF)
    back_out_ref[...] = back_out
    grad_ref[...] = (
        frozen_ref[...].astype(F32) + 0.5 * dot(back_out, out_down_ref[...], TN)
    ).astype(BF)


def attention_kernel(low_ref, q_ref, grad_ref, back_out_ref, query_up_ref, up_ref,
                     out_down_ref, *rest):
    blocks = rest[:SPAN]
    parts_ref, back_query_ref, low_out_ref, query_term_ref, keyval_term_ref, out_term_ref = rest[SPAN : SPAN + 6]
    bias, keys, values, low_keys, low_values, back_parts = rest[SPAN + 6 :]
    position = lax.axis_index("x") * SPAN + lax.axis_index("y")
    own = blocks[0][pl.ds(ROWS, RANK), pl.ds(2 * ROWS, ROWS)][:1]
    own = jnp.broadcast_to(own.astype(F32), (ROWS, ROWS))
    row = lax.broadcasted_iota(jnp.int32, (ROWS, ROWS), 0)
    col = lax.broadcasted_iota(jnp.int32, (ROWS, ROWS), 1)
    for o in range(SPAN):
        span = pl.ds(o * ROWS, ROWS)
        extra = blocks[o][pl.ds(ROWS, RANK), :]
        low_keys[:, span] = extra[:, :ROWS]
        low_values[:, span] = extra[:, ROWS : 2 * ROWS]
        document = jnp.transpose(jnp.broadcast_to(extra[:1, 2 * ROWS : 3 * ROWS].astype(F32), (ROWS, ROWS)))
        seen = own == document
        if o == 0:
            seen = seen & (row <= col)
        else:
            seen = seen & (jnp.broadcast_to(position, (ROWS, ROWS)) >= o)
        one = jnp.where(seen, 0.0, -1e30)
        for i in range(GROUP):
            bias[span, pl.ds(i*ROWS, ROWS)] = one
    back_parts[...] = jnp.zeros_like(back_parts)
    low_zero = low_ref[pl.ds(0, RANK), :]
    back_out = back_out_ref[...]

    def one_group(g, sums):
        back_query, low_out = sums
        at = pl.ds(pl.multiple_of(g * HEAD_SIZE, HEAD_SIZE), HEAD_SIZE)
        value_at = pl.ds(pl.multiple_of(KEY_COLUMNS + g * HEAD_SIZE, HEAD_SIZE), HEAD_SIZE)
        for o in range(SPAN):
            span = pl.ds(o * ROWS, ROWS)
            keys[span, :] = blocks[o][pl.ds(0, ROWS), at]
            values[span, :] = blocks[o][pl.ds(0, ROWS), value_at]
        heads = [pl.ds(pl.multiple_of((g * GROUP + i) * HEAD_SIZE, HEAD_SIZE), HEAD_SIZE) for i in range(GROUP)]
        q = jnp.concatenate([q_ref[:, h] for h in heads], axis=0)
        grad = jnp.concatenate([grad_ref[:, h] for h in heads], axis=0)
        qT = jnp.transpose(q.astype(F32))
        gradT = jnp.transpose(grad.astype(F32))
        k, v = keys[...], values[...]
        scores = dot(k, qT.astype(BF)) * (INVERSE * LOG2E) + bias[...]
        powers = jnp.exp2(scores - jnp.max(scores, axis=0, keepdims=True))
        recip = 1.0 / jnp.sum(powers, axis=0, keepdims=True)
        powers = powers.astype(BF)
        attn = (dot(v, powers, TN) * recip).astype(BF)
        delta = jnp.sum(gradT * attn.astype(F32), axis=0, keepdims=True)
        dprobs = dot(v, gradT.astype(BF))
        dscores = powers * (dprobs - delta).astype(BF)
        dq = (dot(k, dscores, TN) * (recip * INVERSE)).astype(BF)
        scaled_q = jnp.transpose(qT * (recip * INVERSE)).astype(BF)
        scaled_grad = jnp.transpose(gradT * recip).astype(BF)
        dkeys = dot(dscores, scaled_q).astype(BF)
        dvalues = dot(powers, scaled_grad).astype(BF)
        back_parts[pl.ds(0, RANK), :] += dot(up_ref[0, :, at], dkeys, NT)
        back_parts[pl.ds(RANK, RANK), :] += dot(up_ref[1, :, at], dvalues, NT)
        keyval_term_ref[pl.ds(0, RANK), at] = dot(low_keys[...], dkeys)
        keyval_term_ref[pl.ds(RANK, RANK), at] = dot(low_values[...], dvalues)
        for i, h in enumerate(heads):
            mine = slice(i * ROWS, (i + 1) * ROWS)
            query_term_ref[:, h] = dot(low_zero, dq[:, mine], NT)
            out_term_ref[:, h] = dot(back_out, attn[:, mine], NT)
            back_query = back_query + dot(query_up_ref[:, h], dq[:, mine])
            low_out = low_out + dot(out_down_ref[:, h], attn[:, mine])
        return back_query, low_out

    zero = jnp.zeros((RANK, ROWS), F32)
    back_query, low_out = lax.fori_loop(0, KEY_HEADS, one_group, (zero, zero), unroll=True)
    back_query_ref[...] = back_query.astype(BF)
    low_out_ref[...] = low_out.astype(BF)
    parts_ref[...] = jnp.zeros_like(parts_ref)
    for o in range(SPAN):
        parts_ref[lax.rem(position + (DEVICES - o), DEVICES)] = back_parts[:, pl.ds(o * ROWS, ROWS)].astype(BF)


def term_kernel(x_ref, outgrad_ref, back_query_ref, parts_ref, low_out_ref,
                query_term_ref, keyval_term_ref, out_term_ref, kept_ref, sent_ref, both):
    core = lax.axis_index("core")
    back_keyval = parts_ref[0].astype(F32)
    for i in range(1, DEVICES):
        back_keyval = back_keyval + parts_ref[i].astype(F32)
    back = jnp.concatenate([back_query_ref[...], back_keyval.astype(BF)], axis=0)
    down = dot(back, x_ref[...]).astype(BF)
    up = dot(low_out_ref[...], outgrad_ref[...]).astype(BF)
    query_term = query_term_ref[...].astype(BF)
    keyval_term = keyval_term_ref[...].astype(BF)
    out_term = out_term_ref[...].astype(BF)

    def put(half, tile, value):
        both[half, tile // 3, pl.ds(tile % 3 * RANK, RANK), :] = value

    def tiles(half, first, array):
        for t in range(array.shape[1] // ROWS):
            put(half, first + t, array[:, t * ROWS : (t + 1) * ROWS])
        return first + array.shape[1] // ROWS

    first = 0
    for c in range(3):
        first = tiles(0, first, down[c * RANK : (c + 1) * RANK])
    first = tiles(1, 0, query_term)
    first = tiles(1, first, keyval_term[:RANK])
    first = tiles(1, first, keyval_term[RANK:])
    first = tiles(1, first, out_term)
    first = tiles(1, first, up)
    for t in range(first, 96):
        put(1, t, jnp.zeros((RANK, ROWS), BF))
    kept_ref[...] = both[core]
    sent_ref[...] = both[1 - core]


def unpack_kernel(kept_ref, sent_ref, down_ref, query_ref, keyval_ref, out_down_ref, out_up_ref, both):
    core = lax.axis_index("core")
    both[core] = kept_ref[...]
    both[1 - core] = sent_ref[...]

    def get(half, tile):
        return both[half, tile // 3, pl.ds(tile % 3 * RANK, RANK), :]

    for c in range(3):
        for t in range(WIDTH // ROWS):
            down_ref[c, :, pl.ds(t * ROWS, ROWS)] = get(0, c * (WIDTH // ROWS) + t)
    first = 0
    for ref, lead in ((query_ref, None), (keyval_ref, 0), (keyval_ref, 1), (out_down_ref, None), (out_up_ref, None)):
        count = ref.shape[-1] // ROWS
        for t in range(count):
            if lead is None:
                ref[:, pl.ds(t * ROWS, ROWS)] = get(1, first + t)
            else:
                ref[lead, :, pl.ds(t * ROWS, ROWS)] = get(1, first + t)
        first += count


VMEM = pl.BlockSpec(memory_space=pltpu.VMEM)


def call(kernel, name, outs, args, scratch=(), flops=0, size=0, limit=32 << 20, kind=None):
    specs = [kind or VMEM] * len(args)
    return pl.pallas_call(
        kernel,
        name=name,
        out_shape=outs,
        in_specs=specs,
        out_specs=jax.tree.map(lambda _: VMEM, outs),
        scratch_shapes=list(scratch),
        compiler_params=pltpu.CompilerParams(vmem_limit_bytes=limit),
        cost_estimate=pl.CostEstimate(flops=flops, bytes_accessed=size, transcendentals=0),
    )(*args)


def shape(dims, dtype=BF):
    return jax.ShapeDtypeStruct(dims, dtype)


def pairs_up(length, steps):
    return [[(i, i + 1) for i in range(step, length - 1)] for step in range(steps)]


def pairs_down(length, steps):
    last = SPAN - steps
    pairs, wanted = [], {(place - last, place) for place in range(last, length)}
    for offset in range(last + 1, SPAN):
        pairs.insert(0, sorted(((place + 1) % length, place) for _, place in wanted))
        wanted = {(block, (place + 1) % length) for block, place in wanted}
        wanted |= {(place - offset, place) for place in range(offset, length)}
    return [sorted(wanted)] + pairs


def per_device(
    normed_input,
    document_index,
    frozen_query_state,
    frozen_keyvalue_weight,
    layer_output_gradient,
    frozen_output_gradient,
    adapter_down_weight,
    query_up_weight,
    keyvalue_up_weight,
    output_down_weight,
    output_up_weight,
):
    x = normed_input[0]
    outgrad = layer_output_gradient[0]
    down = adapter_down_weight.transpose(0, 2, 1).reshape(3 * RANK, WIDTH)
    out_down = output_down_weight.T
    seq = ("x", "y")
    length = lax.axis_size("x") * lax.axis_size("y")

    low, pack = call(
        keyval_kernel, "keyval", (shape((3 * RANK, ROWS)), shape((PACK_ROWS, 2 * KEY_COLUMNS))),
        (x, down, frozen_keyvalue_weight[0], keyvalue_up_weight, document_index),
        scratch=(
            pltpu.VMEM((ROWS, WIDTH), BF),
            pltpu.VMEM((3 * RANK, WIDTH), BF),
            pltpu.VMEM((ROWS, 2 * KEY_COLUMNS), BF),
            pltpu.VMEM((2, RANK, KEY_COLUMNS), BF),
            pltpu.VMEM((1, ROWS), jnp.int32),
            pltpu.SemaphoreType.DMA((5,)),
        ),
        flops=10**8, size=2 * 10**6, limit=56 << 20, kind=pl.BlockSpec(memory_space=pl.ANY),
    )

    blocks = {0: pack}
    up, down = pairs_up(length, 3), pairs_down(length, 4)
    for step in range(1, 5):
        blocks[8 - step] = lax.ppermute(blocks[(9 - step) % SPAN], seq, down[step - 1])
        if step < 4:
            blocks[step] = lax.ppermute(blocks[step - 1], seq, up[step - 1])

    q, grad, back_out = call(
        query_kernel, "query",
        (shape((ROWS, QUERY_COLUMNS)), shape((ROWS, QUERY_COLUMNS)), shape((RANK, ROWS))),
        (low, frozen_query_state[0], query_up_weight, outgrad, output_up_weight, frozen_output_gradient[0], out_down),
        flops=10**8, size=4 * 10**6,
    )

    window = SPAN * ROWS
    parts, back_query, low_out, query_term, keyval_term, out_term = call(
        attention_kernel, "attention",
        (
            shape((DEVICES, 2 * RANK, ROWS)),
            shape((RANK, ROWS)),
            shape((RANK, ROWS)),
            shape((RANK, QUERY_COLUMNS), F32),
            shape((2 * RANK, KEY_COLUMNS), F32),
            shape((RANK, QUERY_COLUMNS), F32),
        ),
        (low, q, grad, back_out, query_up_weight, keyvalue_up_weight, out_down,
         *[blocks[o] for o in range(SPAN)]),
        scratch=(
            pltpu.VMEM((window, GROUP * ROWS), F32),
            pltpu.VMEM((window, HEAD_SIZE), BF),
            pltpu.VMEM((window, HEAD_SIZE), BF),
            pltpu.VMEM((RANK, window), BF),
            pltpu.VMEM((RANK, window), BF),
            pltpu.VMEM((2 * RANK, window), F32),
        ),
        flops=4 * 10**9, size=4 * 10**6,
    )

    parts = lax.all_to_all(parts, seq, 0, 0, tiled=False)

    half = (length, 3 * RANK, ROWS)
    kept, sent = call(
        term_kernel, "terms", (shape(half), shape(half)),
        (x, outgrad, back_query, parts, low_out, query_term, keyval_term, out_term),
        scratch=(pltpu.VMEM((2, *half), BF),),
        flops=10**8, size=4 * 10**6,
    )

    swap = [(0, 1), (1, 0)]
    total = (kept.astype(F32) + lax.ppermute(sent, "core", swap).astype(F32)).astype(BF)
    total = lax.all_to_all(total, seq, 0, 0, tiled=False)
    total = jnp.sum(total.astype(F32), axis=0).astype(BF)
    depth = lax.axis_size("z")
    total = lax.all_to_all(jnp.broadcast_to(total, (depth, *total.shape)), "z", 0, 0, tiled=False)
    scale = 0.5 / (depth * lax.axis_size("core"))
    total = (jnp.sum(total.astype(F32), axis=0) * scale).astype(BF)
    total = lax.all_to_all(jnp.broadcast_to(total, half), seq, 0, 0, tiled=False)
    other = lax.ppermute(total, "core", swap)

    lora, query_up, keyval_up, output_down, output_up = call(
        unpack_kernel, "unpack",
        (
            shape((3, RANK, WIDTH)),
            shape((RANK, QUERY_COLUMNS)),
            shape((2, RANK, KEY_COLUMNS)),
            shape((RANK, QUERY_COLUMNS)),
            shape((RANK, WIDTH)),
        ),
        (total, other),
        scratch=(pltpu.VMEM((2, *half), BF),),
        size=2 * 10**6,
    )
    return lora.transpose(0, 2, 1), query_up, keyval_up, output_down.T, output_up


def solution(mesh):
    named = Mesh(mesh.devices.reshape(8, 2, 4, 8), ("z", "core", "x", "y"))
    rep, seq = ("z", "core"), ("x", "y")
    split = P(rep, seq, None)
    placed = (split, P(rep, seq), split, split, split, split, P(), P(), P(), P(), P())
    return jax.shard_map(
        per_device, mesh=named, in_specs=placed, out_specs=(P(), P(), P(), P(), P()), check_vma=False
    )
```
